128 devices in a mesh: pipe: 4 (over x), dp: 8 (over y, core), tensor: 4 (over z).
Axes of the slice: x: 4, y: 4, z: 4, core: 2. Of those that a mesh axis runs over, the one named last changes fastest.
Arguments:
- tokens: bfloat16 [4, 2048, 5120], P('pipe', 'dp', 'tensor'), may hold values from -6 to 6
- norm_gain: bfloat16 [4, 5120], P('pipe'), may hold values from 0.099609375 to 1.8984375
- w_query: bfloat16 [4, 5120, 4096], P('pipe', None, 'tensor'), may hold values from -0.078125 to 0.078125
- key_value_weight: bfloat16 [4, 5120, 1024], P('pipe', None, 'tensor'), may hold values from -0.078125 to 0.078125
- w_out: bfloat16 [4, 4096, 5120], P('pipe', 'tensor'), may hold values from -0.5 to 0.5
- cache_kv: bfloat16 [4, 8192, 4, 256], P('pipe', 'dp', 'tensor'), may hold values from -80 to 80
- cache_lengths: int32 [4, 4], P('pipe'), may hold values from 1 to 4096, 8192 in all within a row
- row_lengths: int32 [4, 4], P('pipe'), may hold values from 1 to 1024, 2048 in all within a row
- block_owner: int32 [4, 16, 1], P('pipe'), may hold values from 0 to 7; in each aligned block of 2 rows (0 to 1, 2 to 3, ..., all dimensions but the last counted through in order) no two rows name the same one
Outputs:
- handed: bfloat16 [4, 2048, 5120], P('pipe', 'dp', 'tensor')
- blocks_held: float32 [4, 8], P('pipe', 'dp')
The draws below stay inside these ranges and needn't reach their ends.
Inputs may be any that keep to these rules, and one draw needn't show every extreme that they name: `block_owner`: the 2 aligned row blocks of one data rank at one section hand at most 1 block to any one data rank. `cache_lengths`: each section's documents hold 8192 cached positions in all; the longest exactly 4096. `row_lengths`: each section's documents hold 2048 rows in all; the longest exactly 1024.
All inputs are finite; a program needn't handle non-finite values.
Results may differ from the reference program's by a relative error of at most 0.012.
The reference program's roundings to bfloat16 on the way count: a program that leaves them out, or rounds other values in their place, can miss the bound.
Values may be sent and summed in bfloat16 or wider, within the bound.
A program may use at most 192 MiB of HBM per device.

```python
import math
import jax
import jax.numpy as jnp
import numpy as np
from jax import lax

MODEL_WIDTH = 5120
QUERY_HEADS = 32
LOOKUP_CHANNELS = 4
HEAD_SIZE = 128
BLOCK_ROWS = 128
BLK_DEV = 2
NDOC = 4
HANDOVER_PARTS = 4
HQ_DEV = 8
NBLK = 16
MICRO_ROWS = 2048
STORED_PLACES = 8192
CMAX = 4096
RMAX = 1024
PAIR = 1
N_DP = 8
N_TENSOR = 4


def draw_cache_kv(key, part):
    key = jax.random.fold_in(key, 11)
    extent_size = (HANDOVER_PARTS, STORED_PLACES, LOOKUP_CHANNELS, 2 * HEAD_SIZE)
    key_one = jax.random.fold_in(key, 0)
    element_sequence = jnp.clip(jax.random.normal(key_one, extent_size, jnp.float32), -6.0, 6.0)
    return element_sequence.astype(jnp.bfloat16)


def shard_levels(key, shape, cuts, low, top_value):
    gain = 1.0
    for axis_at, shards_of in cuts:
        draws = jax.random.uniform(jax.random.fold_in(jax.random.fold_in(key, 6), axis_at), (shards_of,), jnp.float32, low / len(cuts), top_value / len(cuts))
        gain = gain * jnp.repeat(jnp.exp(draws), shape[axis_at] // shards_of).reshape((-1,) + (1,) * (len(shape) - 1 - axis_at))
    return gain


def profile(number_of, total, reach, skew):
    portions = [(1 << 20) // math.isqrt(grade ** skew) + 1 for grade in range(2, number_of + 1)]
    spare, given = total - reach - (number_of - 1), [1] * (number_of - 1)
    while spare > 0:
        movable = [i for i in range(number_of - 1) if given[i] < reach]
        pool, left = sum([portions[i] for i in movable]), spare
        for i in movable:
            extra = min(reach - given[i], max(1, left * portions[i] // pool), spare)
            given[i] = given[i] + extra
            spare = spare - extra
    return np.array([reach] + given)


def uneven(rng, count, total, most, skew):
    if count == 2:
        one = jax.random.randint(rng, (), max(1, total - most), min(most, total - 1) + 1)
        return jnp.stack([one, total - one])
    tallies = jnp.asarray(profile(count, total, most, skew), jnp.int32)
    pairs = (count - 1) // 2
    source_of, taker = tallies[1:1 + 2 * pairs:2], tallies[2:2 + 2 * pairs:2]
    slack = jnp.minimum(source_of - 1, most - taker)
    passed = jax.random.randint(jax.random.fold_in(rng, 1), (pairs,), 0, 1 << 20) % (slack + 1)
    tallies = tallies.at[1:1 + 2 * pairs:2].set(source_of - passed).at[2:2 + 2 * pairs:2].set(taker + passed)
    return tallies[jax.random.permutation(jax.random.fold_in(rng, 2), count)]


def routed_block(own_key, own, number, rows, count, top, limit, slope):
    order = jax.random.permutation(own_key, count)
    heavy_load, ordinary = portions_of(count, rows * top, limit, slope, True), portions_of(count, rows * top, limit, slope, False)
    places = jnp.arange(count)

    def named(sizes, turn):
        used = int((sizes > 0).sum())
        fixed = max(1, used // 4)
        moved = fixed + (places - fixed + turn * (used - fixed)) % max(1, count - fixed)
        return jnp.zeros((count,), jnp.int32).at[order[jnp.where(places < fixed, places, moved)]].set(jnp.asarray(sizes, jnp.int32))

    sizes = jnp.where(number % 4 == 0, named(heavy_load, number // 4), named(ordinary, number - number // 4 - 1))
    mixed = jax.random.permutation(jax.random.fold_in(own, 3), count)
    giver, receiver = mixed[0:count // 2 * 2:2], mixed[1:count // 2 * 2:2]
    margin = jnp.minimum(sizes[giver] - 1, limit - sizes[receiver]) // 2
    margin = jnp.where((giver == order[0]) | (receiver == order[0]) | (sizes[receiver] == 0), 0, jnp.maximum(margin, 0))
    moved = jax.random.randint(jax.random.fold_in(own, 4), (count // 2,), 0, 1 << 20) % (margin + 1)
    sizes = sizes.at[giver].add(-moved).at[receiver].add(moved)
    items = jnp.searchsorted(jnp.cumsum(sizes), jnp.arange(rows * top), side="right").astype(jnp.int32)
    grid = items.reshape(top, rows).T
    grid = grid[jax.random.permutation(jax.random.fold_in(own, 1), rows)]
    turn = jax.random.randint(jax.random.fold_in(own, 2), (rows, 1), 0, top)
    return jnp.take_along_axis(grid, (jnp.arange(top)[None, :] + turn) % top, axis=1)


def portions_of(count, total, bound, slope, full):
    portions = [(1 << 20) // math.isqrt(rank ** slope) + 1 for rank in range(1, count + 1)]
    largest = bound if full else min(bound, max(-(-total // count), total * portions[0] // sum(portions)))
    least = 1 if total - largest >= count - 1 else 0
    counts, rest = [largest] + [least] * (count - 1), total - largest - least * (count - 1)
    while rest > 0:
        free = [i for i in range(1, count) if counts[i] < largest] or [i for i in range(1, count) if counts[i] < bound]
        mass, remaining = sum([portions[i] for i in free]), rest
        for i in free:
            more = min(bound - counts[i], max(1, remaining * portions[i] // mass), rest)
            counts[i] = counts[i] + more
            rest = rest - more
    return np.array(counts)


def normal_values(key, dims, width, most, shards=(), kind=jnp.bfloat16):
    values = jax.random.normal(key, dims, jnp.float32) * width
    if len(shards) > 0:
        values = shard_levels(key, dims, shards, -0.22, 0.18) * values
    return jnp.clip(values, min=-most, max=most).astype(kind)


def setup_inputs(seed: int = 0) -> dict:
    keys = jax.random.split(jax.random.key(seed), 10)
    tokens = normal_values(keys[0], (HANDOVER_PARTS, MICRO_ROWS, MODEL_WIDTH), 1.0, 6.0, ((0, 4), (1, 8), (2, 4)))
    norm_gain = jnp.clip(1.0 + 0.18 * jax.random.normal(keys[1], (HANDOVER_PARTS, MODEL_WIDTH), jnp.float32), 0.099609375, 1.8984375).astype(jnp.bfloat16)
    w_query = normal_values(keys[2], (HANDOVER_PARTS, MODEL_WIDTH, QUERY_HEADS * HEAD_SIZE), MODEL_WIDTH ** -0.5, 0.078125, ((0, 4), (2, 4)))
    key_value_weight = normal_values(keys[3], (HANDOVER_PARTS, MODEL_WIDTH, LOOKUP_CHANNELS * 2 * HEAD_SIZE), MODEL_WIDTH ** -0.5, 0.078125, ((0, 4), (2, 4)))
    w_out = normal_values(keys[4], (HANDOVER_PARTS, QUERY_HEADS * HEAD_SIZE, MODEL_WIDTH), HEAD_SIZE ** -0.5, 0.5, ((0, 4), (1, 4)))
    cache_kv = draw_cache_kv(jax.random.fold_in(keys[9], 71), 0)
    cache_lengths = jax.vmap(lambda own: uneven(own, NDOC, STORED_PLACES, CMAX, 2))(jax.random.split(keys[6], HANDOVER_PARTS)).reshape((HANDOVER_PARTS, NDOC)).astype(jnp.int32)
    row_lengths = jax.vmap(lambda own: uneven(own, NDOC, MICRO_ROWS, RMAX, 2))(jax.random.split(keys[7], HANDOVER_PARTS)).reshape((HANDOVER_PARTS, NDOC)).astype(jnp.int32)
    block_owner_keys = jax.random.split(jax.random.fold_in(keys[8], 1), HANDOVER_PARTS * NBLK // BLK_DEV)
    block_owner_turns = jax.random.permutation(jax.random.fold_in(keys[8], 3), HANDOVER_PARTS * NBLK // BLK_DEV)
    block_owner = jax.vmap(lambda own, number: routed_block(jax.random.fold_in(keys[8], 2), own, number, BLK_DEV, N_DP, 1, PAIR, 2))(block_owner_keys, block_owner_turns).reshape((HANDOVER_PARTS, NBLK, 1))
    return {"tokens": tokens, "norm_gain": norm_gain, "w_query": w_query, "key_value_weight": key_value_weight, "w_out": w_out, "cache_kv": cache_kv, "cache_lengths": cache_lengths, "row_lengths": row_lengths, "block_owner": block_owner}


EPS = 1e-06
NEG = -1e+30

def doc_ids(lengths, amount):
    bounds = jnp.cumsum(lengths).astype(jnp.int32)
    places = jnp.arange(amount, dtype=jnp.int32)
    return lax.optimization_barrier(jnp.sum((places[:, None] >= bounds[None, :]).astype(jnp.int32), axis=1))

def block_loads(row_len, cache_len, amount, block_size):
    row_doc = doc_ids(row_len, amount)
    bounds = jnp.cumsum(row_len).astype(jnp.int32)
    starts = bounds - row_len.astype(jnp.int32)
    offsets = cache_len.astype(jnp.int32) - starts + 1
    doc_numbers = jnp.arange(row_len.shape[0], dtype=jnp.int32)
    matches = (row_doc[:, None] == doc_numbers[None, :]).astype(jnp.int32)
    per_row = lax.optimization_barrier(jnp.sum(matches * offsets[None, :], axis=1)) + jnp.arange(amount, dtype=jnp.int32)
    return lax.optimization_barrier(jnp.sum(per_row.reshape(amount // block_size, block_size), axis=1))

def run_section(inputs, gain_row, query_weight, keyval_weight, out_weight, cached_rows, cache_len, row_len):
    widened = inputs.astype(jnp.float32)
    factor = lax.rsqrt(lax.optimization_barrier(jnp.mean(widened * widened, axis=1, keepdims=True)) + EPS)
    normed = (widened * factor * gain_row.astype(jnp.float32)).astype(jnp.bfloat16)
    query_rows = jnp.dot(normed, query_weight, preferred_element_type=jnp.float32).astype(jnp.bfloat16)
    key_value_rows = jnp.dot(normed, keyval_weight, preferred_element_type=jnp.float32).astype(jnp.bfloat16)
    history_rows = jnp.concatenate([cached_rows.reshape(STORED_PLACES, LOOKUP_CHANNELS * 2 * HEAD_SIZE), key_value_rows], axis=0)
    history_rows = history_rows.reshape(STORED_PLACES + MICRO_ROWS, LOOKUP_CHANNELS, 2 * HEAD_SIZE)
    key_part = history_rows[:, :, :HEAD_SIZE].astype(jnp.float32)
    value_part = history_rows[:, :, HEAD_SIZE:].astype(jnp.float32)
    cache_doc = doc_ids(cache_len, STORED_PLACES)
    row_doc = doc_ids(row_len, MICRO_ROWS)
    key_doc = jnp.concatenate([cache_doc, row_doc])
    key_row = jnp.concatenate([jnp.full((STORED_PLACES,), -1, jnp.int32), jnp.arange(MICRO_ROWS, dtype=jnp.int32)])
    group_list = QUERY_HEADS // LOOKUP_CHANNELS
    query_row_blocks = query_rows.reshape(MICRO_ROWS // BLOCK_ROWS, BLOCK_ROWS, LOOKUP_CHANNELS, group_list, HEAD_SIZE)

    def one_block(packed):
        block_query, block_index = packed
        start_row = (block_index * BLOCK_ROWS).astype(jnp.int32)
        own_rows = start_row + jnp.arange(BLOCK_ROWS, dtype=jnp.int32)
        own_docs = lax.dynamic_slice(row_doc, (start_row,), (BLOCK_ROWS,))
        visible = (own_docs[:, None] == key_doc[None, :]) & (key_row[None, :] <= own_rows[:, None])
        visible_wide = visible[:, None, None, :]
        scores = jnp.einsum('qkgd,nkd->qkgn', block_query.astype(jnp.float32), key_part) * HEAD_SIZE ** (-0.5)
        scores = jnp.where(visible_wide, scores, NEG)
        highest = lax.optimization_barrier(jnp.max(scores, axis=3, keepdims=True))
        weights = jnp.where(visible_wide, jnp.exp(scores - highest), 0.0)
        totals = lax.optimization_barrier(jnp.sum(weights, axis=3))
        rounded = lax.optimization_barrier(weights.astype(jnp.bfloat16)).astype(jnp.float32)
        summed = jnp.einsum('qkgn,nkd->qkgd', rounded, value_part)
        return (summed / totals[..., None]).astype(jnp.bfloat16)
    block_numbers = jnp.arange(MICRO_ROWS // BLOCK_ROWS, dtype=jnp.int32)
    attended = lax.map(one_block, (query_row_blocks, block_numbers)).reshape(MICRO_ROWS, QUERY_HEADS * HEAD_SIZE)
    head_width = HQ_DEV * HEAD_SIZE
    partial_sum = jnp.zeros((MICRO_ROWS, MODEL_WIDTH), jnp.float32)
    for group_index in range(N_TENSOR):
        lower = group_index * head_width
        product = jnp.dot(attended[:, lower:lower + head_width], out_weight[lower:lower + head_width], preferred_element_type=jnp.float32)
        partial_sum = partial_sum + lax.optimization_barrier(product.astype(jnp.bfloat16)).astype(jnp.float32)
    return (widened + partial_sum).astype(jnp.bfloat16)

def reference(tokens, norm_gain, w_query, key_value_weight, w_out, cache_kv, cache_lengths, row_lengths, block_owner):
    results = []
    for section_index in range(HANDOVER_PARTS):
        results.append(run_section(tokens[section_index], norm_gain[section_index], w_query[section_index], key_value_weight[section_index], w_out[section_index], cache_kv[section_index], cache_lengths[section_index], row_lengths[section_index]))
    handed = jnp.stack([results[(section_index - 1) % HANDOVER_PARTS] for section_index in range(HANDOVER_PARTS)])
    rank_ids = jnp.arange(N_DP, dtype=jnp.int32)
    loads = jnp.stack([block_loads(row_lengths[section_index], cache_lengths[section_index], MICRO_ROWS, BLOCK_ROWS) for section_index in range(HANDOVER_PARTS)])
    matched = (block_owner[:, :, 0][:, :, None] == rank_ids[None, None, :]).astype(jnp.int32)
    work_sum = lax.optimization_barrier(jnp.sum(matched * loads[:, :, None], axis=1))
    blocks_held = work_sum.astype(jnp.float32) / jnp.float32(BLOCK_ROWS * (CMAX + RMAX))
    return (handed, blocks_held)
```

```python
import functools

import jax
import jax.numpy as jnp
from jax import lax
from jax.experimental import pallas as pl
from jax.experimental.pallas import tpu as pltpu
from jax.sharding import PartitionSpec as P

HEAD = 128
BLOCK = 128
EPS = 1e-06
NEG = -1e30
LOG2E = 1.4426950408889634
MESH = pl.DeviceIdType.MESH
F32 = jnp.float32
BF16 = jnp.bfloat16


def remote(src, dst, sems, index, target):
    return pltpu.make_async_remote_copy(
        src_ref=src,
        dst_ref=dst,
        send_sem=sems[0].at[index],
        recv_sem=sems[1].at[index],
        device_id=target,
        device_id_type=MESH,
    )


def project_kernel(
    n_dp, n_t, tok, gain, wq_hbm, wkv_hbm, cache, q_out, kv_full, cache_full,
    xs, wq, wkv, normed, kv_own, w_sem, loc_sem,
    z_send, z_recv, y_send, y_recv, k_send, k_recv,
):
    rank = lax.axis_index("dp")
    t = lax.axis_index("tensor")
    right, left = lax.rem(t + 1, n_t), lax.rem(t + n_t - 1, n_t)
    over = lax.rem(t + 2, n_t)
    up, down = lax.rem(rank + 2, n_dp), lax.rem(rank + n_dp - 2, n_dp)
    across = lax.rem(rank + 4, n_dp)
    twin = rank + 1 - 2 * lax.rem(rank, 2)
    z, y, k = (z_send, z_recv), (y_send, y_recv), (k_send, k_recv)
    half = BLOCK // 2
    span = cache.shape[0]
    mid = span // 2

    w_copies = [
        pltpu.make_async_copy(wq_hbm, wq, w_sem.at[0]),
        pltpu.make_async_copy(wkv_hbm, wkv, w_sem.at[1]),
    ]

    barrier = pltpu.get_barrier_semaphore()
    for other in (left, right):
        pl.semaphore_signal(barrier, inc=1, device_id={"tensor": other}, device_id_type=MESH)
    for step in range(1, n_dp):
        other = lax.rem(rank + step, n_dp)
        pl.semaphore_signal(barrier, inc=1, device_id={"dp": other}, device_id_type=MESH)
    pl.semaphore_wait(barrier, 2 + n_dp - 1)

    def rows(block, lower, upper):
        return pl.ds(block * BLOCK + lower, upper - lower)

    def z_own(block, way, target):
        part = rows(block, 0, BLOCK)
        return remote(tok.at[part], xs.at[t, part], z, block * 4 + way, {"tensor": target})

    def z_own_in(block, way, source):
        part = xs.at[source, rows(block, 0, BLOCK)]
        return remote(part, part, z, block * 4 + way, {"tensor": source})

    def z_far(block, way, slot, target):
        low = 0 if way == 0 else half
        part = xs.at[slot, rows(block, low, low + half)]
        return remote(part, part, z, block * 4 + 2 + way, {"tensor": target})

    started = []

    def go(copy):
        copy.start()
        started.append(copy)

    go(z_own(0, 0, right))
    go(z_own(0, 1, left))
    go(remote(cache, cache_full.at[rank], y, 0, {"dp": up}))
    go(remote(cache, cache_full.at[rank], y, 1, {"dp": down}))
    go(remote(cache, cache_full.at[rank], y, 4, {"dp": twin}))
    own_cache = pltpu.make_async_copy(cache, cache_full.at[rank], loc_sem.at[0])
    own_cache.start()
    for copy in w_copies:
        copy.start()
    xs[t] = tok[...]

    def y_in(index, slot, lower, upper):
        part = cache_full.at[slot, pl.ds(lower, upper - lower)]
        return remote(part, part, y, index, {"dp": twin})

    def y_out(index, slot, lower, upper, target):
        part = cache_full.at[slot, pl.ds(lower, upper - lower)]
        go(remote(part, part, y, index, {"dp": target}))

    def forward_z(block):
        z_own_in(block, 0, left).wait_recv()
        go(z_far(block, 0, left, right))
        z_own_in(block, 1, right).wait_recv()
        go(z_far(block, 1, right, left))

    def far_z(block):
        z_far(block, 0, over, right).wait_recv()
        z_far(block, 1, over, left).wait_recv()

    def compute(block):
        def norm_rows(step, carry):
            low = pl.multiple_of(block * BLOCK + step * 16, 16)
            low_here = pl.multiple_of(step * 16, 16)
            parts = [xs[i, pl.ds(low, 16), :].astype(F32) for i in range(n_t)]
            total = jnp.sum(parts[0] * parts[0], axis=1, keepdims=True)
            for part in parts[1:]:
                total += jnp.sum(part * part, axis=1, keepdims=True)
            width = parts[0].shape[1]
            factor = lax.rsqrt(total / (width * n_t) + EPS)
            for i, part in enumerate(parts):
                cols = pl.ds(i * width, width)
                scaled = part * factor * gain[:, cols].astype(F32)
                normed[pl.ds(low_here, 16), cols] = scaled.astype(BF16)
            return carry

        lax.fori_loop(0, BLOCK // 16, norm_rows, 0)

        if block == 0:
            w_copies[1].wait()
        made = jnp.dot(normed[...], wkv[...], preferred_element_type=F32)
        kv_own[pl.ds(block * BLOCK, BLOCK), :] = made.astype(BF16)
        part = pl.ds(block * BLOCK, BLOCK)
        for step in range(1, n_dp):
            other = lax.rem(rank + step, n_dp)
            index = block * (n_dp - 1) + step - 1
            go(remote(kv_own.at[part], kv_full.at[rank, part], k, index, {"dp": other}))
        if block == 0:
            w_copies[0].wait()

        def query_tile(n, carry):
            cols = pl.ds(pl.multiple_of(n * 256, 256), 256)
            tile = jnp.dot(normed[...], wq[:, cols], preferred_element_type=F32).astype(BF16)
            q_out[block, 2 * n] = tile[:, :HEAD]
            q_out[block, 2 * n + 1] = tile[:, HEAD:]
            return carry

        lax.fori_loop(0, wq.shape[1] // 256, query_tile, 0)

    forward_z(0)
    go(z_own(1, 0, right))
    go(z_own(1, 1, left))
    far_z(0)
    y_in(0, down, 0, span).wait_recv()
    y_out(2, down, 0, mid, up)
    y_out(5, down, 0, span, twin)
    y_in(1, up, 0, span).wait_recv()
    y_out(3, up, mid, span, down)
    y_out(6, up, 0, span, twin)
    compute(0)
    forward_z(1)
    y_in(2, across, 0, mid).wait_recv()
    y_out(7, across, 0, mid, twin)
    y_in(3, across, mid, span).wait_recv()
    y_out(8, across, mid, span, twin)
    far_z(1)
    compute(1)

    own_kv = pltpu.make_async_copy(kv_own, kv_full.at[rank], loc_sem.at[1])
    own_kv.start()
    twin_of = lambda r: r + 1 - 2 * lax.rem(r, 2)
    y_in(4, twin, 0, span).wait_recv()
    y_in(5, twin_of(down), 0, span).wait_recv()
    y_in(6, twin_of(up), 0, span).wait_recv()
    y_in(7, twin_of(across), 0, mid).wait_recv()
    y_in(8, twin_of(across), mid, span).wait_recv()
    for block in range(2):
        part = pl.ds(block * BLOCK, BLOCK)
        for step in range(1, n_dp):
            source = lax.rem(rank + n_dp - step, n_dp)
            index = block * (n_dp - 1) + step - 1
            here = kv_full.at[source, part]
            remote(here, here, k, index, {"dp": source}).wait_recv()
    own_cache.wait()
    own_kv.wait()
    for copy in started:
        copy.wait_send()


def project(own_rows, gain, w_query, w_kv, cache, n_dp, n_t):
    rows, width = own_rows.shape
    blocks = rows // BLOCK
    full, heads_width = w_query.shape
    kv_width = w_kv.shape[1]
    heads = heads_width // HEAD
    span = cache.shape[0]
    vmem = pl.BlockSpec(memory_space=pltpu.VMEM)
    anywhere = pl.BlockSpec(memory_space=pl.ANY)
    return pl.pallas_call(
        functools.partial(project_kernel, n_dp, n_t),
        out_shape=(
            jax.ShapeDtypeStruct((blocks, heads, BLOCK, HEAD), BF16),
            jax.ShapeDtypeStruct((n_dp, rows, kv_width), BF16),
            jax.ShapeDtypeStruct((n_dp, span, kv_width), BF16),
        ),
        in_specs=[vmem, vmem, anywhere, anywhere, anywhere],
        out_specs=(vmem, anywhere, anywhere),
        scratch_shapes=[
            pltpu.VMEM((n_t, rows, width), BF16),
            pltpu.VMEM((full, heads_width), BF16),
            pltpu.VMEM((full, kv_width), BF16),
            pltpu.VMEM((BLOCK, full), BF16),
            pltpu.VMEM((rows, kv_width), BF16),
            pltpu.SemaphoreType.DMA((2,)),
            pltpu.SemaphoreType.DMA((2,)),
            pltpu.SemaphoreType.DMA((8,)),
            pltpu.SemaphoreType.DMA((8,)),
            pltpu.SemaphoreType.DMA((9,)),
            pltpu.SemaphoreType.DMA((9,)),
            pltpu.SemaphoreType.DMA((2 * (n_dp - 1),)),
            pltpu.SemaphoreType.DMA((2 * (n_dp - 1),)),
        ],
        compiler_params=pltpu.CompilerParams(
            collective_id=0, has_side_effects=True, vmem_limit_bytes=40 * 1024 * 1024
        ),
        name="project",
    )(own_rows, gain, w_query, w_kv, cache)


CHUNK = 512


def attend_kernel(
    n_docs, cache_len, row_len, owner, q, cache, kv, out, held, m_s, l_s, acc_s
):
    rank = lax.axis_index("dp")
    heads = q.shape[1]
    blocks = q.shape[0]
    lanes = heads * BLOCK
    c_len = [cache_len[0, d] for d in range(n_docs)]
    r_len = [row_len[0, d] for d in range(n_docs)]
    r_end, c_end = [], []
    r_sum = c_sum = jnp.int32(0)
    for d in range(n_docs):
        r_sum = r_sum + r_len[d]
        c_sum = c_sum + c_len[d]
        r_end.append(r_sum)
        c_end.append(c_sum)
    r_start = [r_end[d] - r_len[d] for d in range(n_docs)]
    scale = HEAD ** (-0.5) * LOG2E

    def add_where(tests, values):
        total = jnp.where(tests[0], values[0], 0)
        for test, value in zip(tests[1:], values[1:]):
            total = total + jnp.where(test, value, 0)
        return total

    for block in range(blocks):
        first = (rank * blocks + block) * BLOCK
        last = first + BLOCK - 1
        before_first = [r_end[d] <= first for d in range(n_docs)]
        begun = [r_start[d] <= last for d in range(n_docs)]
        c_low = add_where(before_first, c_len)
        c_high = add_where(begun, c_len)
        r_low = add_where(before_first, r_len)
        ended = [r_end[d] <= last for d in range(n_docs)]
        ones = [jnp.int32(1)] * n_docs
        single = add_where(before_first, ones) == add_where(ended, ones)

        row = first + lax.broadcasted_iota(jnp.int32, (1, BLOCK), 1)
        passed = [r_end[d] <= row for d in range(n_docs)]
        reached = [r_start[d] <= row for d in range(n_docs)]
        row_c_low = add_where(passed, c_len)
        row_c_high = add_where(reached, c_len)
        row_r_low = add_where(passed, r_len)

        m_s[...] = jnp.full(m_s.shape, NEG, F32)
        l_s[...] = jnp.zeros(l_s.shape, F32)
        acc_s[...] = jnp.zeros(acc_s.shape, F32)

        def chunk_step(source, start, low_row, high_row, masked):
            keys = source[pl.ds(start, CHUNK), :HEAD]
            values = source[pl.ds(start, CHUNK), HEAD:]
            values_t = values.T
            if masked:
                place = start + lax.broadcasted_iota(jnp.int32, (CHUNK, BLOCK), 0)
                seen = (place >= low_row) & (place < high_row)
            for h in range(0, heads, 2):
                queries = q[block, h : h + 2].reshape(2 * BLOCK, HEAD)
                scores = lax.dot_general(
                    keys, queries, (((1,), (1,)), ((), ())), preferred_element_type=F32
                )
                cols = pl.ds(h * BLOCK, 2 * BLOCK)
                if masked:
                    seen2 = jnp.concatenate([seen, seen], axis=1)
                    scores = jnp.where(seen2, scores, NEG)
                prior = m_s[:, cols]
                newest = jnp.maximum(prior, jnp.max(scores, axis=0, keepdims=True))
                weights = jnp.exp2((scores - newest) * scale)
                if masked:
                    weights = jnp.where(seen2, weights, 0.0)
                rescale = jnp.exp2((prior - newest) * scale)
                m_s[:, cols] = newest
                l_s[:, cols] = l_s[:, cols] * rescale + jnp.sum(weights, axis=0, keepdims=True)
                product = jnp.dot(
                    values_t, weights.astype(BF16), preferred_element_type=F32
                )
                acc_s[:, cols] = acc_s[:, cols] * rescale + product

        def loop_over(source, low, high, low_row, high_row, full_high):
            def one(c, carry):
                start = pl.multiple_of(c * CHUNK, CHUNK)
                whole = single & (start >= low) & (start + CHUNK <= full_high)

                @pl.when(whole)
                def _():
                    chunk_step(source, start, low_row, high_row, False)

                @pl.when(jnp.logical_not(whole))
                def _():
                    chunk_step(source, start, low_row, high_row, True)

                return carry

            lax.fori_loop(low // CHUNK, (high + CHUNK - 1) // CHUNK, one, 0)

        loop_over(cache, c_low, c_high, row_c_low, row_c_high, c_high)
        loop_over(kv, r_low, last + 1, row_r_low, row + 1, first + 1)

        for h in range(heads):
            cols = pl.ds(h * BLOCK, BLOCK)
            done = acc_s[:, cols] / l_s[:, cols]
            out[pl.ds(block * BLOCK, BLOCK), cols] = done.T.astype(BF16)

    def load_of(b, total):
        low = b * BLOCK
        work = low * BLOCK + (BLOCK * (BLOCK - 1)) // 2
        for d in range(n_docs):
            inside = jnp.minimum(r_end[d], low + BLOCK) - jnp.maximum(r_start[d], low)
            work = work + jnp.maximum(inside, 0) * (c_len[d] - r_start[d] + 1)
        return total + jnp.where(owner[b] == rank, work, 0)

    total = lax.fori_loop(0, owner.shape[0], load_of, jnp.int32(0))
    divisor = BLOCK * (cache.shape[0] // 2 + kv.shape[0] // 2)
    held[0, 0] = total.astype(F32) * (1.0 / divisor)


def attend(cache_len, row_len, owner, q, cache, kv):
    blocks, heads = q.shape[:2]
    vmem = pl.BlockSpec(memory_space=pltpu.VMEM)
    smem = pl.BlockSpec(memory_space=pltpu.SMEM)
    return pl.pallas_call(
        functools.partial(attend_kernel, cache_len.shape[1]),
        out_shape=(
            jax.ShapeDtypeStruct((blocks * BLOCK, heads * HEAD), BF16),
            jax.ShapeDtypeStruct((1, 1), F32),
        ),
        in_specs=[smem, smem, smem, vmem, vmem, vmem],
        out_specs=(vmem, smem),
        scratch_shapes=[
            pltpu.VMEM((1, heads * BLOCK), F32),
            pltpu.VMEM((1, heads * BLOCK), F32),
            pltpu.VMEM((HEAD, heads * BLOCK), F32),
        ],
        compiler_params=pltpu.CompilerParams(vmem_limit_bytes=40 * 1024 * 1024),
        name="attend",
    )(cache_len, row_len, owner, q, cache, kv)


PIECES = 4


def output_kernel(
    n_pipe, n_t, att, tok, wo_hbm, out,
    wo, far, far_in, to_right, to_left, own, sent, from_left, from_right, section,
    w_sem, z_send, z_recv, x_send, x_recv,
):
    s = lax.axis_index("pipe")
    t = lax.axis_index("tensor")
    right, left = lax.rem(t + 1, n_t), lax.rem(t + n_t - 1, n_t)
    over = lax.rem(t + 2, n_t)
    ahead, behind = lax.rem(s + 1, n_pipe), lax.rem(s + n_pipe - 1, n_pipe)
    z, x = (z_send, z_recv), (x_send, x_recv)
    width = tok.shape[1]
    size = tok.shape[0] // PIECES
    half = size // 2
    order = (over, right, left, t)
    w_copies = []
    for i, target in enumerate(order):
        cols = pl.ds(pl.multiple_of(target * width, width), width)
        copy = pltpu.make_async_copy(wo_hbm.at[:, cols], wo.at[i], w_sem.at[i])
        copy.start()
        w_copies.append(copy)

    barrier = pltpu.get_barrier_semaphore()
    for other in (left, right):
        pl.semaphore_signal(barrier, inc=1, device_id={"tensor": other}, device_id_type=MESH)
    for other in (ahead, behind):
        pl.semaphore_signal(barrier, inc=1, device_id={"pipe": other}, device_id_type=MESH)
    pl.semaphore_wait(barrier, 4)

    def multiply(i, store):
        w_copies[i].wait()

        def tile(n, carry):
            cols = pl.ds(pl.multiple_of(n * 256, 256), 256)
            store(cols, jnp.dot(att[...], wo[i, :, cols], preferred_element_type=F32))
            return carry

        lax.fori_loop(0, width // 256, tile, 0)

    started = []

    def go(copy):
        copy.start()
        started.append(copy)

    def span(p, way):
        return pl.ds(p * size + way * half, half)

    def far_copy(p, way):
        target = right if way == 0 else left
        return remote(far.at[span(p, way)], far_in.at[span(p, way)], z, p * 6 + way, {"tensor": target})

    def near_copy(p, way, kind):
        part = span(p, way if kind == 1 else 1 - way)
        target, box = (right, from_left) if way == 0 else (left, from_right)
        return remote(sent.at[way, part], box.at[part], z, p * 6 + 2 + 2 * kind + way, {"tensor": target})

    def store_far(cols, value):
        far[:, cols] = value.astype(BF16)

    multiply(0, store_far)
    for p in range(PIECES):
        for way in range(2):
            go(far_copy(p, way))

    def store_right(cols, value):
        to_right[:, cols] = value

    def store_left(cols, value):
        to_left[:, cols] = value

    multiply(1, store_right)
    multiply(2, store_left)
    held = (to_right, to_left)
    for p in range(PIECES):
        for way in range(2):
            part = span(p, 1 - way)
            sent[way, part, :] = held[way][part, :].astype(BF16)
            go(near_copy(p, way, 0))
        for way in range(2):
            part = span(p, way)
            far_copy(p, way).wait_recv()
            sent[way, part, :] = (held[way][part, :] + far_in[part, :].astype(F32)).astype(BF16)
            go(near_copy(p, way, 1))

    def store_own(cols, value):
        own[:, cols] = value + tok[:, cols].astype(F32)

    multiply(3, store_own)
    for p in range(PIECES):
        for way in range(2):
            near_copy(p, way, 0).wait_recv()
            near_copy(p, way, 1).wait_recv()
        part = pl.ds(p * size, size)
        total = from_left[part, :].astype(F32) + from_right[part, :].astype(F32)
        section[part, :] = (own[part, :] + total).astype(BF16)
        go(remote(section.at[part], out.at[part], x, p, {"pipe": ahead}))
    for p in range(PIECES):
        part = pl.ds(p * size, size)
        remote(section.at[part], out.at[part], x, p, {"pipe": ahead}).wait_recv()
    for copy in started:
        copy.wait_send()


def output(att, own_rows, w_out, n_pipe, n_t):
    rows, width = own_rows.shape
    vmem = pl.BlockSpec(memory_space=pltpu.VMEM)
    anywhere = pl.BlockSpec(memory_space=pl.ANY)
    whole = (rows, width)
    return pl.pallas_call(
        functools.partial(output_kernel, n_pipe, n_t),
        out_shape=jax.ShapeDtypeStruct(whole, BF16),
        in_specs=[vmem, vmem, anywhere],
        out_specs=anywhere,
        scratch_shapes=[
            pltpu.VMEM((n_t, w_out.shape[0], width), BF16),
            pltpu.VMEM(whole, BF16),
            pltpu.VMEM(whole, BF16),
            pltpu.VMEM(whole, F32),
            pltpu.VMEM(whole, F32),
            pltpu.VMEM(whole, F32),
            pltpu.VMEM((2,) + whole, BF16),
            pltpu.VMEM(whole, BF16),
            pltpu.VMEM(whole, BF16),
            pltpu.VMEM(whole, BF16),
            pltpu.SemaphoreType.DMA((n_t,)),
            pltpu.SemaphoreType.DMA((6 * PIECES,)),
            pltpu.SemaphoreType.DMA((6 * PIECES,)),
            pltpu.SemaphoreType.DMA((PIECES,)),
            pltpu.SemaphoreType.DMA((PIECES,)),
        ],
        compiler_params=pltpu.CompilerParams(
            collective_id=1, has_side_effects=True, vmem_limit_bytes=40 * 1024 * 1024
        ),
        name="output",
    )(att, own_rows, w_out)


def on_device(
    tokens, norm_gain, w_query, key_value_weight, w_out, cache_kv,
    cache_lengths, row_lengths, block_owner,
):
    n_pipe, n_dp, n_t = (lax.axis_size(a) for a in ("pipe", "dp", "tensor"))
    own_rows = tokens[0]
    span = cache_kv.shape[1]
    cache = cache_kv.reshape(span, cache_kv.shape[3])
    q, kv_full, cache_full = project(
        own_rows, norm_gain, w_query[0], key_value_weight[0], cache, n_dp, n_t
    )
    kv_width = kv_full.shape[2]
    att, held = attend(
        cache_lengths, row_lengths, block_owner.reshape(-1), q,
        cache_full.reshape(-1, kv_width), kv_full.reshape(-1, kv_width),
    )
    handed = output(att, own_rows, w_out[0], n_pipe, n_t)
    return handed[None], held


def solution(mesh):
    placed = (
        P("pipe", "dp", "tensor"),
        P("pipe", None),
        P("pipe", None, "tensor"),
        P("pipe", None, "tensor"),
        P("pipe", "tensor", None),
        P("pipe", "dp", "tensor", None),
        P("pipe", None),
        P("pipe", None),
        P("pipe", None, None),
    )
    return jax.shard_map(
        on_device,
        mesh=mesh,
        in_specs=placed,
        out_specs=(P("pipe", "dp", "tensor"), P("pipe", "dp")),
        check_vma=False,
    )
```

```python
import functools

import jax
import jax.numpy as jnp
from jax import lax
from jax.experimental import pallas as pl
from jax.experimental.pallas import tpu as pltpu
from jax.sharding import PartitionSpec as P

HEAD = 128
BLOCK = 128
EPS = 1e-06
NEG = -1e30
LOG2E = 1.4426950408889634
MESH = pl.DeviceIdType.MESH
F32 = jnp.float32
BF16 = jnp.bfloat16


def remote(src, dst, sems, index, target):
    return pltpu.make_async_remote_copy(
        src_ref=src,
        dst_ref=dst,
        send_sem=sems[0].at[index],
        recv_sem=sems[1].at[index],
        device_id=target,
        device_id_type=MESH,
    )


def project_kernel(
    n_dp, n_t, tok, gain_hbm, wq_hbm, wkv_hbm, cache, q_out, hist,
    xs, gain, wq, wkv, normed, kv_own, w_sem, loc_sem,
    z_send, z_recv, y_send, y_recv, k_send, k_recv,
):
    rank = lax.axis_index("dp")
    t = lax.axis_index("tensor")
    right, left = lax.rem(t + 1, n_t), lax.rem(t + n_t - 1, n_t)
    over = lax.rem(t + 2, n_t)
    up, down = lax.rem(rank + 2, n_dp), lax.rem(rank + n_dp - 2, n_dp)
    across = lax.rem(rank + 4, n_dp)
    twin = rank + 1 - 2 * lax.rem(rank, 2)
    z, y, k = (z_send, z_recv), (y_send, y_recv), (k_send, k_recv)
    half = BLOCK // 2
    span = cache.shape[0]
    mid = span // 2
    fresh = span * n_dp

    def cached_at(slot, lower, upper):
        return hist.at[pl.ds(pl.multiple_of(slot * span + lower, mid), upper - lower)]

    def fresh_at(slot, lower, upper):
        place = fresh + slot * kv_own.shape[0] + lower
        return hist.at[pl.ds(pl.multiple_of(place, BLOCK), upper - lower)]

    w_copies = [
        pltpu.make_async_copy(wq_hbm, wq, w_sem.at[0]),
        pltpu.make_async_copy(wkv_hbm, wkv, w_sem.at[1]),
        pltpu.make_async_copy(gain_hbm, gain, w_sem.at[2]),
    ]

    barrier = pltpu.get_barrier_semaphore()
    for other in (left, right):
        pl.semaphore_signal(barrier, inc=1, device_id={"tensor": other}, device_id_type=MESH)
    for step in range(1, n_dp):
        other = lax.rem(rank + step, n_dp)
        pl.semaphore_signal(barrier, inc=1, device_id={"dp": other}, device_id_type=MESH)
    pl.semaphore_wait(barrier, 2 + n_dp - 1)

    def rows(block, lower, upper):
        return pl.ds(block * BLOCK + lower, upper - lower)

    def z_own(block, way, target):
        part = rows(block, 0, BLOCK)
        return remote(tok.at[part], xs.at[t, part], z, block * 4 + way, {"tensor": target})

    def z_own_in(block, way, source):
        part = xs.at[source, rows(block, 0, BLOCK)]
        return remote(part, part, z, block * 4 + way, {"tensor": source})

    def z_far(block, way, slot, target):
        low = 0 if way == 0 else half
        part = xs.at[slot, rows(block, low, low + half)]
        return remote(part, part, z, block * 4 + 2 + way, {"tensor": target})

    started = []

    def go(copy):
        copy.start()
        started.append(copy)

    go(z_own(0, 0, right))
    go(z_own(0, 1, left))
    go(remote(cache, cached_at(rank, 0, span), y, 0, {"dp": up}))
    go(remote(cache, cached_at(rank, 0, span), y, 1, {"dp": down}))
    go(remote(cache, cached_at(rank, 0, span), y, 4, {"dp": twin}))
    own_cache = pltpu.make_async_copy(cache, cached_at(rank, 0, span), loc_sem.at[0])
    own_cache.start()
    for copy in w_copies:
        copy.start()
    own_tok = pltpu.make_async_copy(tok, xs.at[t], loc_sem.at[2])
    own_tok.start()

    def y_in(index, slot, lower, upper):
        part = cached_at(slot, lower, upper)
        return remote(part, part, y, index, {"dp": twin})

    def y_out(index, slot, lower, upper, target):
        part = cached_at(slot, lower, upper)
        go(remote(part, part, y, index, {"dp": target}))

    def forward_z(block):
        z_own_in(block, 0, left).wait_recv()
        go(z_far(block, 0, left, right))
        z_own_in(block, 1, right).wait_recv()
        go(z_far(block, 1, right, left))

    def far_z(block):
        z_far(block, 0, over, right).wait_recv()
        z_far(block, 1, over, left).wait_recv()

    def compute(block):
        def norm_rows(step, carry):
            low = pl.multiple_of(block * BLOCK + step * 16, 16)
            low_here = pl.multiple_of(step * 16, 16)
            parts = [xs[i, pl.ds(low, 16), :].astype(F32) for i in range(n_t)]
            total = jnp.sum(parts[0] * parts[0], axis=1, keepdims=True)
            for part in parts[1:]:
                total += jnp.sum(part * part, axis=1, keepdims=True)
            width = parts[0].shape[1]
            factor = lax.rsqrt(total / (width * n_t) + EPS)
            for i, part in enumerate(parts):
                cols = pl.ds(i * width, width)
                scaled = part * factor * gain[:, cols].astype(F32)
                normed[pl.ds(low_here, 16), cols] = scaled.astype(BF16)
            return carry

        if block == 0:
            w_copies[2].wait()
        lax.fori_loop(0, BLOCK // 16, norm_rows, 0)

        if block == 0:
            w_copies[1].wait()
        made = jnp.dot(normed[...], wkv[...], preferred_element_type=F32)
        kv_own[pl.ds(block * BLOCK, BLOCK), :] = made.astype(BF16)
        part = pl.ds(block * BLOCK, BLOCK)
        for step in range(1, n_dp):
            other = lax.rem(rank + step, n_dp)
            index = block * (n_dp - 1) + step - 1
            here = fresh_at(rank, block * BLOCK, block * BLOCK + BLOCK)
            go(remote(kv_own.at[part], here, k, index, {"dp": other}))
        if block == 0:
            w_copies[0].wait()

        def query_tile(n, carry):
            cols = pl.ds(pl.multiple_of(n * 256, 256), 256)
            tile = jnp.dot(normed[...], wq[:, cols], preferred_element_type=F32).astype(BF16)
            q_out[block, 2 * n] = tile[:, :HEAD]
            q_out[block, 2 * n + 1] = tile[:, HEAD:]
            return carry

        lax.fori_loop(0, wq.shape[1] // 256, query_tile, 0)

    forward_z(0)
    own_tok.wait()
    go(z_own(1, 0, right))
    go(z_own(1, 1, left))
    far_z(0)
    y_in(0, down, 0, span).wait_recv()
    y_out(2, down, 0, mid, up)
    y_out(5, down, 0, span, twin)
    y_in(1, up, 0, span).wait_recv()
    y_out(3, up, mid, span, down)
    y_out(6, up, 0, span, twin)
    compute(0)
    forward_z(1)
    y_in(2, across, 0, mid).wait_recv()
    y_out(7, across, 0, mid, twin)
    y_in(3, across, mid, span).wait_recv()
    y_out(8, across, mid, span, twin)
    far_z(1)
    compute(1)

    own_kv = pltpu.make_async_copy(kv_own, fresh_at(rank, 0, kv_own.shape[0]), loc_sem.at[1])
    own_kv.start()
    twin_of = lambda r: r + 1 - 2 * lax.rem(r, 2)
    y_in(4, twin, 0, span).wait_recv()
    y_in(5, twin_of(down), 0, span).wait_recv()
    y_in(6, twin_of(up), 0, span).wait_recv()
    y_in(7, twin_of(across), 0, mid).wait_recv()
    y_in(8, twin_of(across), mid, span).wait_recv()
    for block in range(2):
        for step in range(1, n_dp):
            source = lax.rem(rank + n_dp - step, n_dp)
            index = block * (n_dp - 1) + step - 1
            here = fresh_at(source, block * BLOCK, block * BLOCK + BLOCK)
            remote(here, here, k, index, {"dp": source}).wait_recv()
    own_cache.wait()
    own_kv.wait()
    for copy in started:
        copy.wait_send()


def project(own_rows, gain, w_query, w_kv, cache, n_dp, n_t):
    rows, width = own_rows.shape
    blocks = rows // BLOCK
    full, heads_width = w_query.shape
    kv_width = w_kv.shape[1]
    heads = heads_width // HEAD
    span = cache.shape[0]
    vmem = pl.BlockSpec(memory_space=pltpu.VMEM)
    hbm = pl.BlockSpec(memory_space=pltpu.HBM)
    return pl.pallas_call(
        functools.partial(project_kernel, n_dp, n_t),
        out_shape=(
            jax.ShapeDtypeStruct((blocks, heads, BLOCK, HEAD), BF16),
            jax.ShapeDtypeStruct((n_dp * (span + rows), kv_width), BF16),
        ),
        in_specs=[hbm] * 5,
        out_specs=(vmem, pl.BlockSpec(memory_space=pltpu.VMEM)),
        scratch_shapes=[
            pltpu.VMEM((n_t, rows, width), BF16),
            pltpu.VMEM(gain.shape, BF16),
            pltpu.VMEM((full, heads_width), BF16),
            pltpu.VMEM((full, kv_width), BF16),
            pltpu.VMEM((BLOCK, full), BF16),
            pltpu.VMEM((rows, kv_width), BF16),
            pltpu.SemaphoreType.DMA((3,)),
            pltpu.SemaphoreType.DMA((3,)),
            pltpu.SemaphoreType.DMA((8,)),
            pltpu.SemaphoreType.DMA((8,)),
            pltpu.SemaphoreType.DMA((9,)),
            pltpu.SemaphoreType.DMA((9,)),
            pltpu.SemaphoreType.DMA((2 * (n_dp - 1),)),
            pltpu.SemaphoreType.DMA((2 * (n_dp - 1),)),
        ],
        compiler_params=pltpu.CompilerParams(
            collective_id=0, has_side_effects=True, vmem_limit_bytes=40 * 1024 * 1024
        ),
        name="project",
    )(*(pltpu.with_memory_space_constraint(a, pltpu.HBM) for a in (own_rows, gain, w_query, w_kv, cache)))


class Layout:
    def __init__(self, cache_len, row_len, n_docs):
        self.n = n_docs
        self.c_len = [cache_len[0, d] for d in range(n_docs)]
        self.r_len = [row_len[0, d] for d in range(n_docs)]
        self.r_start, self.r_end = [], []
        total = jnp.int32(0)
        for length in self.r_len:
            self.r_start.append(total)
            total = total + length
            self.r_end.append(total)

    def _sum(self, tests, values):
        total = jnp.where(tests[0], values[0], 0)
        for test, value in zip(tests[1:], values[1:]):
            total = total + jnp.where(test, value, 0)
        return total

    def ranges(self, first, last):
        past = [end <= first for end in self.r_end]
        begun = [start <= last for start in self.r_start]
        return self._sum(past, self.c_len), self._sum(begun, self.c_len), self._sum(past, self.r_len)


def lane_rows(first):
    return first + lax.broadcasted_iota(jnp.int32, (1, BLOCK), 1)


def align_down(value):
    return value // 16 * 16


def reset_state(m_s, l_s, acc_s):
    m_s[...] = jnp.full(m_s.shape, NEG, F32)
    l_s[...] = jnp.zeros(l_s.shape, F32)
    acc_s[...] = jnp.zeros(acc_s.shape, F32)


def attend_chunk(hist, start, size, low, high, queries, m_s, l_s, acc_s):
    scale = HEAD ** (-0.5) * LOG2E
    place0 = jnp.minimum(start, hist.shape[0] - size)
    at = pl.ds(pl.multiple_of(place0, 16), size)
    keys = hist[at, :HEAD]
    values_t = hist[at, HEAD:].T
    place = place0 + lax.broadcasted_iota(jnp.int32, (size, BLOCK), 0)
    bias = jnp.where((place >= jnp.maximum(low, start)) & (place < high), 0.0, 2 * NEG)
    bias = jnp.concatenate([bias, bias], axis=1)
    heads = len(queries)
    scores = []
    for h in range(0, heads, 2):
        pair = jnp.concatenate([queries[h], queries[h + 1]], axis=0)
        scores.append(
            lax.dot_general(keys, pair, (((1,), (1,)), ((), ())), preferred_element_type=F32)
        )
    weighted = []
    for i, score in enumerate(scores):
        cols = pl.ds(i * 2 * BLOCK, 2 * BLOCK)
        score = score + bias
        prior = m_s[:, cols]
        newest = jnp.maximum(prior, jnp.max(score, axis=0, keepdims=True))
        weights = jnp.exp2((score - newest) * scale)
        rescale = jnp.exp2((prior - newest) * scale)
        m_s[:, cols] = newest
        l_s[:, cols] = l_s[:, cols] * rescale + jnp.sum(weights, axis=0, keepdims=True)
        weighted.append((weights.astype(BF16), rescale))
    for i, (weights, rescale) in enumerate(weighted):
        cols = pl.ds(i * 2 * BLOCK, 2 * BLOCK)
        product = jnp.dot(values_t, weights, preferred_element_type=F32)
        acc_s[:, cols] = acc_s[:, cols] * rescale + product


def finish_block(heads, m_s, l_s, acc_s, store):
    for h in range(heads):
        cols = pl.ds(h * BLOCK, BLOCK)
        store(cols, (acc_s[:, cols] / l_s[:, cols]).T.astype(BF16))


CHUNK = 1024


def attend_kernel(
    n_docs, cached, cache_len, row_len, owner, q, hist, out, held, m_s, l_s, acc_s
):
    rank = lax.axis_index("dp")
    blocks, heads = q.shape[:2]
    layout = Layout(cache_len, row_len, n_docs)

    def one_block(block, carry):
        first = (rank * blocks + block) * BLOCK
        c_low, c_high, r_low = layout.ranges(first, first + BLOCK - 1)
        row = lane_rows(first)
        row_c_low, row_c_high, row_r_low = layout.ranges(row, row)
        reset_state(m_s, l_s, acc_s)
        queries = [q[block, h] for h in range(heads)]

        def one_range(part, carry):
            new = part == 1
            low = jnp.where(new, cached + r_low, c_low)
            high = jnp.where(new, cached + first + BLOCK, c_high)
            lane_low = jnp.where(new, cached + row_r_low, row_c_low)
            lane_high = jnp.where(new, cached + row + 1, row_c_high)
            begin = align_down(low)
            total = high - begin
            whole = total // CHUNK
            rest = total - whole * CHUNK

            def one(k, carry):
                attend_chunk(
                    hist, begin + k * CHUNK, CHUNK, lane_low, lane_high, queries, m_s, l_s, acc_s
                )
                return carry

            lax.fori_loop(0, whole + (rest > CHUNK // 2).astype(jnp.int32), one, 0)

            @pl.when((rest > 0) & (rest <= CHUNK // 2))
            def _():
                attend_chunk(
                    hist, begin + whole * CHUNK, CHUNK // 2, lane_low, lane_high, queries,
                    m_s, l_s, acc_s,
                )

            return carry

        lax.fori_loop(0, 2, one_range, 0)

        def store(cols, value):
            out[pl.ds(pl.multiple_of(block * BLOCK, BLOCK), BLOCK), cols] = value

        finish_block(heads, m_s, l_s, acc_s, store)
        return carry

    lax.fori_loop(0, blocks, one_block, 0)

    def load_of(b, total):
        low = b * BLOCK
        work = low * BLOCK + (BLOCK * (BLOCK - 1)) // 2
        for d in range(n_docs):
            inside = jnp.minimum(layout.r_end[d], low + BLOCK) - jnp.maximum(layout.r_start[d], low)
            gain = layout.c_len[d] - layout.r_start[d] + 1
            work = work + jnp.maximum(inside, 0) * gain
        return total + jnp.where(owner[b] == rank, work, 0)

    total = lax.fori_loop(0, owner.shape[0], load_of, jnp.int32(0))
    held[0, 0] = total.astype(F32) * (1.0 / (BLOCK * (hist.shape[0] // 2)))


def attend(cache_len, row_len, owner, q, hist, cached):
    blocks, heads = q.shape[:2]
    vmem = pl.BlockSpec(memory_space=pltpu.VMEM)
    smem = pl.BlockSpec(memory_space=pltpu.SMEM)
    return pl.pallas_call(
        functools.partial(attend_kernel, cache_len.shape[1], cached),
        out_shape=(
            jax.ShapeDtypeStruct((blocks * BLOCK, heads * HEAD), BF16),
            jax.ShapeDtypeStruct((1, 1), F32),
        ),
        in_specs=[smem, smem, smem, vmem, vmem],
        out_specs=(vmem, smem),
        scratch_shapes=[
            pltpu.VMEM((1, heads * BLOCK), F32),
            pltpu.VMEM((1, heads * BLOCK), F32),
            pltpu.VMEM((HEAD, heads * BLOCK), F32),
        ],
        compiler_params=pltpu.CompilerParams(vmem_limit_bytes=40 * 1024 * 1024),
        name="attend",
    )(cache_len, row_len, owner, q, hist)


PIECES = 4


def output_kernel(
    n_pipe, n_t, att, tok, wo, out,
    far, far_in, to_right, to_left, own, sent, from_left, from_right, section,
    z_send, z_recv, x_send, x_recv,
):
    s = lax.axis_index("pipe")
    t = lax.axis_index("tensor")
    right, left = lax.rem(t + 1, n_t), lax.rem(t + n_t - 1, n_t)
    over = lax.rem(t + 2, n_t)
    ahead, behind = lax.rem(s + 1, n_pipe), lax.rem(s + n_pipe - 1, n_pipe)
    z, x = (z_send, z_recv), (x_send, x_recv)
    width = tok.shape[1]
    size = tok.shape[0] // PIECES
    half = size // 2
    barrier = pltpu.get_barrier_semaphore()
    for other in (left, right):
        pl.semaphore_signal(barrier, inc=1, device_id={"tensor": other}, device_id_type=MESH)
    for other in (ahead, behind):
        pl.semaphore_signal(barrier, inc=1, device_id={"pipe": other}, device_id_type=MESH)
    pl.semaphore_wait(barrier, 4)

    def multiply(target, store):
        def tile(n, carry):
            cols = pl.ds(pl.multiple_of(n * 256, 256), 256)
            out_cols = pl.ds(pl.multiple_of(target * width + n * 256, 256), 256)
            store(cols, jnp.dot(att[...], wo[:, out_cols], preferred_element_type=F32))
            return carry

        lax.fori_loop(0, width // 256, tile, 0)

    started = []

    def go(copy):
        copy.start()
        started.append(copy)

    def span(p, way):
        return pl.ds(p * size + way * half, half)

    def far_copy(p, way):
        target = right if way == 0 else left
        return remote(far.at[span(p, way)], far_in.at[span(p, way)], z, p * 6 + way, {"tensor": target})

    def near_copy(p, way, kind):
        part = span(p, way if kind == 1 else 1 - way)
        target, box = (right, from_left) if way == 0 else (left, from_right)
        return remote(sent.at[way, part], box.at[part], z, p * 6 + 2 + 2 * kind + way, {"tensor": target})

    def store_far(cols, value):
        far[:, cols] = value.astype(BF16)

    multiply(over, store_far)
    for p in range(PIECES):
        for way in range(2):
            go(far_copy(p, way))

    def store_right(cols, value):
        to_right[:, cols] = value

    def store_left(cols, value):
        to_left[:, cols] = value

    multiply(right, store_right)
    multiply(left, store_left)
    held = (to_right, to_left)
    for p in range(PIECES):
        for way in range(2):
            part = span(p, 1 - way)
            sent[way, part, :] = held[way][part, :].astype(BF16)
            go(near_copy(p, way, 0))
        for way in range(2):
            part = span(p, way)
            far_copy(p, way).wait_recv()
            sent[way, part, :] = (held[way][part, :] + far_in[part, :].astype(F32)).astype(BF16)
            go(near_copy(p, way, 1))

    def store_own(cols, value):
        own[:, cols] = value + tok[:, cols].astype(F32)

    multiply(t, store_own)
    for p in range(PIECES):
        for way in range(2):
            near_copy(p, way, 0).wait_recv()
            near_copy(p, way, 1).wait_recv()
        part = pl.ds(p * size, size)
        total = from_left[part, :].astype(F32) + from_right[part, :].astype(F32)
        section[part, :] = (own[part, :] + total).astype(BF16)
        go(remote(section.at[part], out.at[part], x, p, {"pipe": ahead}))
    for p in range(PIECES):
        part = pl.ds(p * size, size)
        remote(section.at[part], out.at[part], x, p, {"pipe": ahead}).wait_recv()
    for copy in started:
        copy.wait_send()


def output(att, own_rows, w_out, n_pipe, n_t):
    rows, width = own_rows.shape
    vmem = pl.BlockSpec(memory_space=pltpu.VMEM)
    anywhere = pl.BlockSpec(memory_space=pl.ANY)
    whole = (rows, width)
    return pl.pallas_call(
        functools.partial(output_kernel, n_pipe, n_t),
        out_shape=jax.ShapeDtypeStruct(whole, BF16),
        in_specs=[vmem, vmem, vmem],
        out_specs=anywhere,
        scratch_shapes=[
            pltpu.VMEM(whole, BF16),
            pltpu.VMEM(whole, BF16),
            pltpu.VMEM(whole, F32),
            pltpu.VMEM(whole, F32),
            pltpu.VMEM(whole, F32),
            pltpu.VMEM((2,) + whole, BF16),
            pltpu.VMEM(whole, BF16),
            pltpu.VMEM(whole, BF16),
            pltpu.VMEM(whole, BF16),
            pltpu.SemaphoreType.DMA((6 * PIECES,)),
            pltpu.SemaphoreType.DMA((6 * PIECES,)),
            pltpu.SemaphoreType.DMA((PIECES,)),
            pltpu.SemaphoreType.DMA((PIECES,)),
        ],
        compiler_params=pltpu.CompilerParams(
            collective_id=1, has_side_effects=True, vmem_limit_bytes=40 * 1024 * 1024
        ),
        name="output",
    )(att, own_rows, w_out)


def on_device(
    tokens, norm_gain, w_query, key_value_weight, w_out, cache_kv,
    cache_lengths, row_lengths, block_owner,
):
    n_pipe, n_dp, n_t = (lax.axis_size(a) for a in ("pipe", "dp", "tensor"))
    own_rows = tokens[0]
    span = cache_kv.shape[1]
    cache = cache_kv.reshape(span, cache_kv.shape[3])
    q, hist = project(
        own_rows, norm_gain, w_query[0], key_value_weight[0], cache, n_dp, n_t
    )
    att, held = attend(
        cache_lengths, row_lengths, block_owner.reshape(-1), q, hist, span * n_dp
    )
    handed = output(att, own_rows, w_out[0], n_pipe, n_t)
    return handed[None], held


def solution(mesh):
    placed = (
        P("pipe", "dp", "tensor"),
        P("pipe", None),
        P("pipe", None, "tensor"),
        P("pipe", None, "tensor"),
        P("pipe", "tensor", None),
        P("pipe", "dp", "tensor", None),
        P("pipe", None),
        P("pipe", None),
        P("pipe", None, None),
    )
    return jax.shard_map(
        on_device,
        mesh=mesh,
        in_specs=placed,
        out_specs=(P("pipe", "dp", "tensor"), P("pipe", "dp")),
        check_vma=False,
    )
```

```python
import functools

import jax
import jax.numpy as jnp
from jax import lax
from jax.experimental import pallas as pl
from jax.experimental.pallas import tpu as pltpu
from jax.sharding import PartitionSpec as P

HEAD = 128
BLOCK = 128
EPS = 1e-06
NEG = -1e30
LOG2E = 1.4426950408889634
MESH = pl.DeviceIdType.MESH
F32 = jnp.float32
BF16 = jnp.bfloat16


def remote(src, dst, sems, index, target):
    return pltpu.make_async_remote_copy(
        src_ref=src,
        dst_ref=dst,
        send_sem=sems[0].at[index],
        recv_sem=sems[1].at[index],
        device_id=target,
        device_id_type=MESH,
    )


class Layout:
    def __init__(self, cache_len, row_len, n_docs):
        self.n = n_docs
        self.c_len = [cache_len[0, d] for d in range(n_docs)]
        self.r_len = [row_len[0, d] for d in range(n_docs)]
        self.r_start, self.r_end = [], []
        total = jnp.int32(0)
        for length in self.r_len:
            self.r_start.append(total)
            total = total + length
            self.r_end.append(total)

    def _sum(self, tests, values):
        total = jnp.where(tests[0], values[0], 0)
        for test, value in zip(tests[1:], values[1:]):
            total = total + jnp.where(test, value, 0)
        return total

    def ranges(self, first, last):
        past = [end <= first for end in self.r_end]
        begun = [start <= last for start in self.r_start]
        return self._sum(past, self.c_len), self._sum(begun, self.c_len), self._sum(past, self.r_len)


def lane_rows(first):
    return first + lax.broadcasted_iota(jnp.int32, (1, BLOCK), 1)


def align_down(value):
    return lax.div(value, 16) * 16


def reset_state(m_s, l_s, acc_s):
    m_s[...] = jnp.full(m_s.shape, NEG, F32)
    l_s[...] = jnp.zeros(l_s.shape, F32)
    acc_s[...] = jnp.zeros(acc_s.shape, F32)


def attend_chunk(hist, start, size, low, high, queries, m_s, l_s, acc_s):
    scale = HEAD ** (-0.5) * LOG2E
    place0 = jnp.minimum(lax.div(start, 16), (hist.shape[0] - size) // 16) * 16
    at = pl.ds(place0, size)
    keys = hist[at, :HEAD]
    values_t = hist[at, HEAD:].T
    place = place0 + lax.broadcasted_iota(jnp.int32, (size, BLOCK), 0)
    bias = jnp.where((place >= jnp.maximum(low, start)) & (place < high), 0.0, 2 * NEG)
    bias = jnp.concatenate([bias, bias], axis=1)
    heads = len(queries)
    scores = []
    for h in range(0, heads, 2):
        pair = jnp.concatenate([queries[h], queries[h + 1]], axis=0)
        scores.append(
            lax.dot_general(keys, pair, (((1,), (1,)), ((), ())), preferred_element_type=F32)
        )
    weighted = []
    for i, score in enumerate(scores):
        cols = pl.ds(i * 2 * BLOCK, 2 * BLOCK)
        score = score + bias
        prior = m_s[:, cols]
        newest = jnp.maximum(prior, jnp.max(score, axis=0, keepdims=True))
        weights = jnp.exp2((score - newest) * scale)
        rescale = jnp.exp2((prior - newest) * scale)
        m_s[:, cols] = newest
        l_s[:, cols] = l_s[:, cols] * rescale + jnp.sum(weights, axis=0, keepdims=True)
        weighted.append((weights.astype(BF16), rescale))
    for i, (weights, rescale) in enumerate(weighted):
        cols = pl.ds(i * 2 * BLOCK, 2 * BLOCK)
        product = jnp.dot(values_t, weights, preferred_element_type=F32)
        acc_s[:, cols] = acc_s[:, cols] * rescale + product


def finish_block(heads, m_s, l_s, acc_s, store):
    for h in range(heads):
        cols = pl.ds(h * BLOCK, BLOCK)
        store(cols, (acc_s[:, cols] / l_s[:, cols]).T.astype(BF16))


CHUNK = 1024
EARLY = 4

def project_kernel(
    n_dp, n_t, n_docs, tok, gain_hbm, wq_hbm, wkv_hbm, cache, cache_len, row_len,
    q_out, cache_all, kv_all, m_s, l_s, acc_s,
    xs, gain, wq, wkv, normed, kv_own, w_sem, loc_sem,
    z_send, z_recv, y_send, y_recv, k_send, k_recv,
):
    rank = lax.axis_index("dp")
    t = lax.axis_index("tensor")
    right, left = lax.rem(t + 1, n_t), lax.rem(t + n_t - 1, n_t)
    over = lax.rem(t + 2, n_t)
    up, down = lax.rem(rank + 2, n_dp), lax.rem(rank + n_dp - 2, n_dp)
    across = lax.rem(rank + 4, n_dp)

    def twin_of(r):
        return r + 1 - 2 * lax.rem(r, 2)

    twin = twin_of(rank)
    z, y, k = (z_send, z_recv), (y_send, y_recv), (k_send, k_recv)
    half = BLOCK // 2
    span = cache.shape[0]
    mid = span // 2
    held = kv_own.shape[0]
    heads = q_out.shape[1]

    def cached_at(slot, lower, upper):
        return cache_all.at[pl.ds(pl.multiple_of(slot * span + lower, mid), upper - lower)]

    def fresh_at(slot, block):
        return kv_all.at[pl.ds(pl.multiple_of(slot * held + block * BLOCK, BLOCK), BLOCK)]

    w_copies = [
        pltpu.make_async_copy(wq_hbm, wq, w_sem.at[0]),
        pltpu.make_async_copy(wkv_hbm, wkv, w_sem.at[1]),
        pltpu.make_async_copy(gain_hbm, gain, w_sem.at[2]),
    ]
    own_tok = pltpu.make_async_copy(tok, xs.at[t], loc_sem.at[2])
    own_cache = pltpu.make_async_copy(cache, cached_at(rank, 0, span), loc_sem.at[0])

    barrier = pltpu.get_barrier_semaphore()
    for other in (left, right):
        pl.semaphore_signal(barrier, inc=1, device_id={"tensor": other}, device_id_type=MESH)
    for other in (up, down, across, twin):
        pl.semaphore_signal(barrier, inc=1, device_id={"dp": other}, device_id_type=MESH)
    own_tok.start()
    own_cache.start()
    for copy in w_copies:
        copy.start()
    pl.semaphore_wait(barrier, 6)

    started = []

    def go(copy):
        copy.start()
        started.append(copy)

    def rows(block, way, kind):
        low = block * BLOCK + (half if (way == 0) == (kind == 1) else 0)
        return pl.ds(low, half)

    def z_go(block, way, kind):
        part = rows(block, way, kind)
        target, source = (right, left) if way == 0 else (left, right)
        slot = source if kind == 2 else t
        src = xs.at[slot, part] if kind == 2 else tok.at[part]
        index = block * 6 + way * 3 + kind
        go(remote(src, xs.at[slot, part], z, index, {"tensor": target}))

    def z_take(block, way, kind):
        source = left if way == 0 else right
        slot = over if kind == 2 else source
        here = xs.at[slot, rows(block, way, kind)]
        index = block * 6 + way * 3 + kind
        remote(here, here, z, index, {"tensor": source}).wait_recv()

    def y_take(index, slot, lower, upper):
        part = cached_at(slot, lower, upper)
        remote(part, part, y, index, {"dp": twin}).wait_recv()

    def y_go(index, slot, lower, upper, target):
        part = cached_at(slot, lower, upper)
        go(remote(part, part, y, index, {"dp": target}))

    def k_start(block):
        part = kv_own.at[pl.ds(block * BLOCK, BLOCK)]
        for i, target in enumerate((up, down, across, twin)):
            go(remote(part, fresh_at(rank, block), k, block * 7 + i, {"dp": target}))

    def k_take(index, slot, block):
        here = fresh_at(slot, block)
        remote(here, here, k, index, {"dp": twin}).wait_recv()

    def k_pass_on(block):
        for i, slot in enumerate((down, up, across)):
            k_take(block * 7 + i, slot, block)
            here = fresh_at(slot, block)
            go(remote(here, here, k, block * 7 + 4 + i, {"dp": twin}))

    def k_finish(block):
        k_take(block * 7 + 3, twin, block)
        for i, slot in enumerate((down, up, across)):
            k_take(block * 7 + 4 + i, twin_of(slot), block)

    def project_block(block):
        def norm_rows(step, carry):
            low = pl.multiple_of(block * BLOCK + step * 16, 16)
            low_here = pl.multiple_of(step * 16, 16)
            parts = [xs[i, pl.ds(low, 16), :].astype(F32) for i in range(n_t)]
            total = jnp.sum(parts[0] * parts[0], axis=1, keepdims=True)
            for part in parts[1:]:
                total += jnp.sum(part * part, axis=1, keepdims=True)
            width = parts[0].shape[1]
            factor = lax.rsqrt(total / (width * n_t) + EPS)
            for i, part in enumerate(parts):
                cols = pl.ds(i * width, width)
                scaled = part * factor * gain[:, cols].astype(F32)
                normed[pl.ds(low_here, 16), cols] = scaled.astype(BF16)
            return carry

        if block == 0:
            w_copies[2].wait()
        lax.fori_loop(0, BLOCK // 16, norm_rows, 0)
        if block == 0:
            w_copies[1].wait()
        made = jnp.dot(normed[...], wkv[...], preferred_element_type=F32)
        kv_own[pl.ds(block * BLOCK, BLOCK), :] = made.astype(BF16)
        k_start(block)
        if block == 0:
            w_copies[0].wait()

        def query_tile(n, carry):
            cols = pl.ds(pl.multiple_of(n * 256, 256), 256)
            tile = jnp.dot(normed[...], wq[:, cols], preferred_element_type=F32).astype(BF16)
            q_out[block, 2 * n] = tile[:, :HEAD]
            q_out[block, 2 * n + 1] = tile[:, HEAD:]
            return carry

        lax.fori_loop(0, wq.shape[1] // 256, query_tile, 0)

    for way in range(2):
        z_go(0, way, 0)
    for way in range(2):
        z_go(0, way, 1)
    go(remote(cache, cached_at(rank, 0, span), y, 0, {"dp": up}))
    go(remote(cache, cached_at(rank, 0, span), y, 1, {"dp": down}))
    go(remote(cache, cached_at(rank, 0, span), y, 4, {"dp": twin}))
    reset_state(m_s, l_s, acc_s)
    layout = Layout(cache_len, row_len, n_docs)
    first = rank * held
    c_low, c_high, r_low = layout.ranges(first, first + BLOCK - 1)
    row = lane_rows(first)
    lane_low, lane_high, lane_r_low = layout.ranges(row, row)

    for way in range(2):
        z_take(0, way, 0)
        z_go(0, way, 2)
    for way in range(2):
        z_go(1, way, 0)
    for way in range(2):
        z_go(1, way, 1)
    own_tok.wait()
    for way in range(2):
        z_take(0, way, 1)
        z_take(0, way, 2)
    y_take(0, down, 0, span)
    y_go(2, down, 0, mid, up)
    y_go(5, down, 0, span, twin)
    y_take(1, up, 0, span)
    y_go(3, up, mid, span, down)
    y_go(6, up, 0, span, twin)
    project_block(0)
    for way in range(2):
        z_take(1, way, 0)
        z_go(1, way, 2)
    y_take(2, across, 0, mid)
    y_go(7, across, 0, mid, twin)
    y_take(3, across, mid, span)
    y_go(8, across, mid, span, twin)
    k_pass_on(0)
    own_cache.wait()
    y_take(4, twin, 0, span)
    y_take(5, twin_of(down), 0, span)
    y_take(6, twin_of(up), 0, span)
    y_take(7, twin_of(across), 0, mid)
    y_take(8, twin_of(across), mid, span)

    def early(c, carry):
        queries = [q_out[0, h] for h in range(heads)]
        start = align_down(c_low) + c * CHUNK
        attend_chunk(cache_all, start, CHUNK, lane_low, lane_high, queries, m_s, l_s, acc_s)
        return carry

    lax.fori_loop(0, EARLY // 2, early, 0)
    for way in range(2):
        z_take(1, way, 1)
        z_take(1, way, 2)
    project_block(1)
    own_kv = pltpu.make_async_copy(
        kv_own, kv_all.at[pl.ds(pl.multiple_of(rank * held, held), held)], loc_sem.at[1]
    )
    own_kv.start()
    k_pass_on(1)
    lax.fori_loop(EARLY // 2, EARLY, early, 0)
    for block in range(2):
        k_finish(block)
    own_kv.wait()
    for copy in started:
        copy.wait_send()


def project(own_rows, gain, w_query, w_kv, cache, cache_len, row_len, n_dp, n_t):
    rows, width = own_rows.shape
    blocks = rows // BLOCK
    full, heads_width = w_query.shape
    kv_width = w_kv.shape[1]
    heads = heads_width // HEAD
    span = cache.shape[0]
    vmem = pl.BlockSpec(memory_space=pltpu.VMEM)
    smem = pl.BlockSpec(memory_space=pltpu.SMEM)
    hbm = pl.BlockSpec(memory_space=pltpu.HBM)
    large = (own_rows, gain, w_query, w_kv, cache)
    return pl.pallas_call(
        functools.partial(project_kernel, n_dp, n_t, cache_len.shape[1]),
        out_shape=(
            jax.ShapeDtypeStruct((blocks, heads, BLOCK, HEAD), BF16),
            jax.ShapeDtypeStruct((n_dp * span, kv_width), BF16),
            jax.ShapeDtypeStruct((n_dp * rows, kv_width), BF16),
            jax.ShapeDtypeStruct((1, heads * BLOCK), F32),
            jax.ShapeDtypeStruct((1, heads * BLOCK), F32),
            jax.ShapeDtypeStruct((HEAD, heads * BLOCK), F32),
        ),
        in_specs=[hbm] * len(large) + [smem] * 2,
        out_specs=(vmem,) * 6,
        scratch_shapes=[
            pltpu.VMEM((n_t, rows, width), BF16),
            pltpu.VMEM(gain.shape, BF16),
            pltpu.VMEM((full, heads_width), BF16),
            pltpu.VMEM((full, kv_width), BF16),
            pltpu.VMEM((BLOCK, full), BF16),
            pltpu.VMEM((rows, kv_width), BF16),
            pltpu.SemaphoreType.DMA((3,)),
            pltpu.SemaphoreType.DMA((3,)),
            pltpu.SemaphoreType.DMA((12,)),
            pltpu.SemaphoreType.DMA((12,)),
            pltpu.SemaphoreType.DMA((9,)),
            pltpu.SemaphoreType.DMA((9,)),
            pltpu.SemaphoreType.DMA((14,)),
            pltpu.SemaphoreType.DMA((14,)),
        ],
        compiler_params=pltpu.CompilerParams(
            collective_id=0, has_side_effects=True, vmem_limit_bytes=40 * 1024 * 1024
        ),
        name="project",
    )(*(pltpu.with_memory_space_constraint(a, pltpu.HBM) for a in large + (cache_len, row_len)))


def attend_kernel(
    n_docs, cache_len, row_len, owner, q, cache, kv, m_in, l_in, acc_in, out, held, m_s, l_s, acc_s
):
    rank = lax.axis_index("dp")
    blocks, heads = q.shape[:2]
    layout = Layout(cache_len, row_len, n_docs)

    def one_block(block, carry):
        first = (rank * blocks + block) * BLOCK
        c_low, c_high, r_low = layout.ranges(first, first + BLOCK - 1)
        row = lane_rows(first)
        row_c_low, row_c_high, row_r_low = layout.ranges(row, row)
        queries = [q[block, h] for h in range(heads)]
        done = jnp.where(block == 0, EARLY, 0)

        @pl.when(block == 0)
        def _():
            m_s[...] = m_in[...]
            l_s[...] = l_in[...]
            acc_s[...] = acc_in[...]

        @pl.when(block > 0)
        def _():
            reset_state(m_s, l_s, acc_s)

        def one_range(source, low, high, lane_low, lane_high, done):
            begin = align_down(low)
            total = high - begin
            whole = total // CHUNK
            rest = total - whole * CHUNK

            def one(c, carry):
                start = begin + c * CHUNK
                attend_chunk(source, start, CHUNK, lane_low, lane_high, queries, m_s, l_s, acc_s)
                return carry

            lax.fori_loop(done, whole + (rest > CHUNK // 2).astype(jnp.int32), one, 0)

            @pl.when((rest > 0) & (rest <= CHUNK // 2) & (whole >= done))
            def _():
                start = begin + whole * CHUNK
                attend_chunk(
                    source, start, CHUNK // 2, lane_low, lane_high, queries, m_s, l_s, acc_s
                )

        one_range(cache, c_low, c_high, row_c_low, row_c_high, done)
        one_range(kv, r_low, first + BLOCK, row_r_low, row + 1, 0)

        def store(cols, value):
            out[pl.ds(pl.multiple_of(block * BLOCK, BLOCK), BLOCK), cols] = value

        finish_block(heads, m_s, l_s, acc_s, store)
        return carry

    lax.fori_loop(0, blocks, one_block, 0)

    def load_of(b, total):
        low = b * BLOCK
        work = low * BLOCK + (BLOCK * (BLOCK - 1)) // 2
        for d in range(n_docs):
            inside = jnp.minimum(layout.r_end[d], low + BLOCK) - jnp.maximum(layout.r_start[d], low)
            gain = layout.c_len[d] - layout.r_start[d] + 1
            work = work + jnp.maximum(inside, 0) * gain
        return total + jnp.where(owner[b] == rank, work, 0)

    total = lax.fori_loop(0, owner.shape[0], load_of, jnp.int32(0))
    held[0, 0] = total.astype(F32) * (2.0 / (BLOCK * (cache.shape[0] + kv.shape[0])))


def attend(cache_len, row_len, owner, q, cache, kv, state):
    blocks, heads = q.shape[:2]
    vmem = pl.BlockSpec(memory_space=pltpu.VMEM)
    smem = pl.BlockSpec(memory_space=pltpu.SMEM)
    return pl.pallas_call(
        functools.partial(attend_kernel, cache_len.shape[1]),
        out_shape=(
            jax.ShapeDtypeStruct((blocks * BLOCK, heads * HEAD), BF16),
            jax.ShapeDtypeStruct((1, 1), F32),
        ),
        in_specs=[smem] * 3 + [vmem] * 6,
        out_specs=(vmem, smem),
        scratch_shapes=[pltpu.VMEM(part.shape, F32) for part in state],
        compiler_params=pltpu.CompilerParams(vmem_limit_bytes=40 * 1024 * 1024),
        name="attend",
    )(cache_len, row_len, owner, q, cache, kv, *state)


PIECES = 4


def output_kernel(
    n_pipe, n_t, att, tok, wo, out,
    far, far_in, to_right, to_left, own, sent, from_left, from_right, section,
    z_send, z_recv, x_send, x_recv,
):
    s = lax.axis_index("pipe")
    t = lax.axis_index("tensor")
    right, left = lax.rem(t + 1, n_t), lax.rem(t + n_t - 1, n_t)
    over = lax.rem(t + 2, n_t)
    ahead, behind = lax.rem(s + 1, n_pipe), lax.rem(s + n_pipe - 1, n_pipe)
    z, x = (z_send, z_recv), (x_send, x_recv)
    width = tok.shape[1]
    size = tok.shape[0] // PIECES
    half = size // 2
    barrier = pltpu.get_barrier_semaphore()
    for other in (left, right):
        pl.semaphore_signal(barrier, inc=1, device_id={"tensor": other}, device_id_type=MESH)
    for other in (ahead, behind):
        pl.semaphore_signal(barrier, inc=1, device_id={"pipe": other}, device_id_type=MESH)
    pl.semaphore_wait(barrier, 4)

    def multiply(target, store):
        def tile(n, carry):
            cols = pl.ds(pl.multiple_of(n * 256, 256), 256)
            out_cols = pl.ds(pl.multiple_of(target * width + n * 256, 256), 256)
            store(cols, jnp.dot(att[...], wo[:, out_cols], preferred_element_type=F32))
            return carry

        lax.fori_loop(0, width // 256, tile, 0)

    started = []

    def go(copy):
        copy.start()
        started.append(copy)

    def span(p, way):
        return pl.ds(p * size + way * half, half)

    def far_copy(p, way):
        target = right if way == 0 else left
        return remote(far.at[span(p, way)], far_in.at[span(p, way)], z, p * 6 + way, {"tensor": target})

    def near_copy(p, way, kind):
        part = span(p, way if kind == 1 else 1 - way)
        target, box = (right, from_left) if way == 0 else (left, from_right)
        return remote(sent.at[way, part], box.at[part], z, p * 6 + 2 + 2 * kind + way, {"tensor": target})

    def store_far(cols, value):
        far[:, cols] = value.astype(BF16)

    multiply(over, store_far)
    for p in range(PIECES):
        for way in range(2):
            go(far_copy(p, way))

    def store_right(cols, value):
        to_right[:, cols] = value

    def store_left(cols, value):
        to_left[:, cols] = value

    multiply(right, store_right)
    multiply(left, store_left)
    held = (to_right, to_left)
    for p in range(PIECES):
        for way in range(2):
            part = span(p, 1 - way)
            sent[way, part, :] = held[way][part, :].astype(BF16)
            go(near_copy(p, way, 0))
        for way in range(2):
            part = span(p, way)
            far_copy(p, way).wait_recv()
            sent[way, part, :] = (held[way][part, :] + far_in[part, :].astype(F32)).astype(BF16)
            go(near_copy(p, way, 1))

    def store_own(cols, value):
        own[:, cols] = value + tok[:, cols].astype(F32)

    multiply(t, store_own)
    for p in range(PIECES):
        for way in range(2):
            near_copy(p, way, 0).wait_recv()
            near_copy(p, way, 1).wait_recv()
        part = pl.ds(p * size, size)
        total = from_left[part, :].astype(F32) + from_right[part, :].astype(F32)
        section[part, :] = (own[part, :] + total).astype(BF16)
        go(remote(section.at[part], out.at[part], x, p, {"pipe": ahead}))
    for p in range(PIECES):
        part = pl.ds(p * size, size)
        remote(section.at[part], out.at[part], x, p, {"pipe": ahead}).wait_recv()
    for copy in started:
        copy.wait_send()


def output(att, own_rows, w_out, n_pipe, n_t):
    rows, width = own_rows.shape
    vmem = pl.BlockSpec(memory_space=pltpu.VMEM)
    anywhere = pl.BlockSpec(memory_space=pl.ANY)
    whole = (rows, width)
    return pl.pallas_call(
        functools.partial(output_kernel, n_pipe, n_t),
        out_shape=jax.ShapeDtypeStruct(whole, BF16),
        in_specs=[vmem, vmem, vmem],
        out_specs=anywhere,
        scratch_shapes=[
            pltpu.VMEM(whole, BF16),
            pltpu.VMEM(whole, BF16),
            pltpu.VMEM(whole, F32),
            pltpu.VMEM(whole, F32),
            pltpu.VMEM(whole, F32),
            pltpu.VMEM((2,) + whole, BF16),
            pltpu.VMEM(whole, BF16),
            pltpu.VMEM(whole, BF16),
            pltpu.VMEM(whole, BF16),
            pltpu.SemaphoreType.DMA((6 * PIECES,)),
            pltpu.SemaphoreType.DMA((6 * PIECES,)),
            pltpu.SemaphoreType.DMA((PIECES,)),
            pltpu.SemaphoreType.DMA((PIECES,)),
        ],
        compiler_params=pltpu.CompilerParams(
            collective_id=1, has_side_effects=True, vmem_limit_bytes=40 * 1024 * 1024
        ),
        name="output",
    )(att, own_rows, w_out)


def on_device(
    tokens, norm_gain, w_query, key_value_weight, w_out, cache_kv,
    cache_lengths, row_lengths, block_owner,
):
    n_pipe, n_dp, n_t = (lax.axis_size(a) for a in ("pipe", "dp", "tensor"))
    own_rows = tokens[0]
    span = cache_kv.shape[1]
    cache = cache_kv.reshape(span, cache_kv.shape[3])
    q, cache_all, kv_all, *state = project(
        own_rows, norm_gain, w_query[0], key_value_weight[0], cache,
        cache_lengths, row_lengths, n_dp, n_t,
    )
    owner = block_owner.reshape(-1)
    att, held = attend(cache_lengths, row_lengths, owner, q, cache_all, kv_all, state)
    handed = output(att, own_rows, w_out[0], n_pipe, n_t)
    return handed[None], held


def solution(mesh):
    placed = (
        P("pipe", "dp", "tensor"),
        P("pipe", None),
        P("pipe", None, "tensor"),
        P("pipe", None, "tensor"),
        P("pipe", "tensor", None),
        P("pipe", "dp", "tensor", None),
        P("pipe", None),
        P("pipe", None),
        P("pipe", None, None),
    )
    return jax.shard_map(
        on_device,
        mesh=mesh,
        in_specs=placed,
        out_specs=(P("pipe", "dp", "tensor"), P("pipe", "dp")),
        check_vma=False,
    )
```

```python
import functools

import jax
import jax.numpy as jnp
from jax import lax
from jax.experimental import pallas as pl
from jax.experimental.pallas import tpu as pltpu
from jax.sharding import PartitionSpec as P

HEAD = 128
BLOCK = 128
EPS = 1e-06
NEG = -1e30
LOG2E = 1.4426950408889634
MESH = pl.DeviceIdType.MESH
F32 = jnp.float32
BF16 = jnp.bfloat16


def remote(src, dst, sems, index, target):
    return pltpu.make_async_remote_copy(
        src_ref=src,
        dst_ref=dst,
        send_sem=sems[0].at[index],
        recv_sem=sems[1].at[index],
        device_id=target,
        device_id_type=MESH,
    )


class Layout:
    def __init__(self, cache_len, row_len, n_docs):
        self.n = n_docs
        self.c_len = [cache_len[0, d] for d in range(n_docs)]
        self.r_len = [row_len[0, d] for d in range(n_docs)]
        self.r_start, self.r_end = [], []
        total = jnp.int32(0)
        for length in self.r_len:
            self.r_start.append(total)
            total = total + length
            self.r_end.append(total)

    def _sum(self, tests, values):
        total = jnp.where(tests[0], values[0], 0)
        for test, value in zip(tests[1:], values[1:]):
            total = total + jnp.where(test, value, 0)
        return total

    def ranges(self, first, last):
        past = [end <= first for end in self.r_end]
        begun = [start <= last for start in self.r_start]
        return self._sum(past, self.c_len), self._sum(begun, self.c_len), self._sum(past, self.r_len)


def lane_rows(first):
    return first + lax.broadcasted_iota(jnp.int32, (1, BLOCK), 1)


def align_down(value):
    return lax.div(value, 16) * 16


def reset_state(m_s, l_s, acc_s):
    m_s[...] = jnp.full(m_s.shape, NEG, F32)
    l_s[...] = jnp.zeros(l_s.shape, F32)
    acc_s[...] = jnp.zeros(acc_s.shape, F32)


def attend_chunk(hist, start, size, low, high, queries, m_s, l_s, acc_s):
    scale = HEAD ** (-0.5) * LOG2E
    place0 = jnp.minimum(lax.div(start, 16), (hist.shape[0] - size) // 16) * 16
    at = pl.ds(place0, size)
    keys = hist[at, :HEAD]
    values_t = hist[at, HEAD:].T
    place = place0 + lax.broadcasted_iota(jnp.int32, (size, BLOCK), 0)
    bias = jnp.where((place >= jnp.maximum(low, start)) & (place < high), 0.0, 2 * NEG)
    bias = jnp.concatenate([bias, bias], axis=1)
    heads = len(queries)
    scores = []
    for h in range(0, heads, 2):
        pair = jnp.concatenate([queries[h], queries[h + 1]], axis=0)
        scores.append(
            lax.dot_general(keys, pair, (((1,), (1,)), ((), ())), preferred_element_type=F32)
        )
    weighted = []
    for i, score in enumerate(scores):
        cols = pl.ds(i * 2 * BLOCK, 2 * BLOCK)
        score = score + bias
        prior = m_s[:, cols]
        newest = jnp.maximum(prior, jnp.max(score, axis=0, keepdims=True))
        weights = jnp.exp2((score - newest) * scale)
        rescale = jnp.exp2((prior - newest) * scale)
        m_s[:, cols] = newest
        l_s[:, cols] = l_s[:, cols] * rescale + jnp.sum(weights, axis=0, keepdims=True)
        weighted.append((weights.astype(BF16), rescale))
    for i, (weights, rescale) in enumerate(weighted):
        cols = pl.ds(i * 2 * BLOCK, 2 * BLOCK)
        product = jnp.dot(values_t, weights, preferred_element_type=F32)
        acc_s[:, cols] = acc_s[:, cols] * rescale + product


def finish_block(heads, out, m_s, l_s, acc_s):
    for h in range(heads):
        cols = pl.ds(h * BLOCK, BLOCK)
        out[:, cols] = (acc_s[:, cols] / l_s[:, cols]).T.astype(BF16)


CHUNK = 1024
EARLY = 4
LATE = 4

def project_kernel(
    n_dp, n_t, n_docs, tok, gain_hbm, wq_hbm, wkv_hbm, cache, cache_len, row_len,
    q_out, cache_all, kv_all, m_s, l_s, acc_s,
    xs, gain, wq, wkv, normed, kv_own, w_sem, loc_sem,
    z_send, z_recv, y_send, y_recv, k_send, k_recv,
):
    s = lax.axis_index("pipe")
    rank = lax.axis_index("dp")
    t = lax.axis_index("tensor")
    right, left = lax.rem(t + 1, n_t), lax.rem(t + n_t - 1, n_t)
    over = lax.rem(t + 2, n_t)
    up, down = lax.rem(rank + 2, n_dp), lax.rem(rank + n_dp - 2, n_dp)
    across = lax.rem(rank + 4, n_dp)

    def twin_of(r):
        return r + 1 - 2 * lax.rem(r, 2)

    twin = twin_of(rank)
    z, y, k = (z_send, z_recv), (y_send, y_recv), (k_send, k_recv)
    half = BLOCK // 2
    span = cache.shape[0]
    mid = span // 2
    held = kv_own.shape[0]
    heads = q_out.shape[1]

    def cached_at(slot, lower, upper):
        return cache_all.at[pl.ds(pl.multiple_of(slot * span + lower, mid), upper - lower)]

    def fresh_at(slot, block):
        return kv_all.at[pl.ds(pl.multiple_of(slot * held + block * BLOCK, BLOCK), BLOCK)]

    w_copies = [
        pltpu.make_async_copy(wq_hbm, wq, w_sem.at[0]),
        pltpu.make_async_copy(wkv_hbm, wkv, w_sem.at[1]),
        pltpu.make_async_copy(gain_hbm, gain, w_sem.at[2]),
    ]
    own_tok = pltpu.make_async_copy(tok, xs.at[t], loc_sem.at[2])
    own_cache = pltpu.make_async_copy(cache, cached_at(rank, 0, span), loc_sem.at[0])

    barrier = pltpu.get_barrier_semaphore()
    for other in (left, right):
        pl.semaphore_signal(barrier, inc=1, device_id=(s, rank, other), device_id_type=MESH)
    for other in (up, down, across, twin):
        pl.semaphore_signal(barrier, inc=1, device_id=(s, other, t), device_id_type=MESH)
    own_tok.start()
    own_cache.start()
    for copy in w_copies:
        copy.start()
    pl.semaphore_wait(barrier, 6)

    started = []

    def go(copy):
        copy.start()
        started.append(copy)

    def rows(block, way, kind):
        low = block * BLOCK + (half if (way == 0) == (kind == 1) else 0)
        return pl.ds(low, half)

    def z_go(block, way, kind):
        part = rows(block, way, kind)
        target, source = (right, left) if way == 0 else (left, right)
        slot = source if kind == 2 else t
        src = xs.at[slot, part] if kind == 2 else tok.at[part]
        index = block * 6 + way * 3 + kind
        go(remote(src, xs.at[slot, part], z, index, (s, rank, target)))

    def z_take(block, way, kind):
        source = left if way == 0 else right
        slot = over if kind == 2 else source
        here = xs.at[slot, rows(block, way, kind)]
        index = block * 6 + way * 3 + kind
        remote(here, here, z, index, (s, rank, source)).wait_recv()

    def y_take(index, slot, lower, upper):
        part = cached_at(slot, lower, upper)
        remote(part, part, y, index, (s, twin, t)).wait_recv()

    def y_go(index, slot, lower, upper, target):
        part = cached_at(slot, lower, upper)
        go(remote(part, part, y, index, (s, target, t)))

    def k_start(block):
        part = kv_own.at[pl.ds(block * BLOCK, BLOCK)]
        for i, target in enumerate((up, down, across, twin)):
            go(remote(part, fresh_at(rank, block), k, block * 7 + i, (s, target, t)))

    def k_take(index, slot, block):
        here = fresh_at(slot, block)
        remote(here, here, k, index, (s, twin, t)).wait_recv()

    def k_pass_on(block):
        for i, slot in enumerate((down, up, across)):
            k_take(block * 7 + i, slot, block)
            here = fresh_at(slot, block)
            go(remote(here, here, k, block * 7 + 4 + i, (s, twin, t)))

    def k_finish(block):
        k_take(block * 7 + 3, twin, block)
        for i, slot in enumerate((down, up, across)):
            k_take(block * 7 + 4 + i, twin_of(slot), block)

    def project_block(block):
        def norm_rows(step, carry):
            low = pl.multiple_of(block * BLOCK + step * 16, 16)
            low_here = pl.multiple_of(step * 16, 16)
            parts = [xs[i, pl.ds(low, 16), :].astype(F32) for i in range(n_t)]
            total = jnp.sum(parts[0] * parts[0], axis=1, keepdims=True)
            for part in parts[1:]:
                total += jnp.sum(part * part, axis=1, keepdims=True)
            width = parts[0].shape[1]
            factor = lax.rsqrt(total / (width * n_t) + EPS)
            for i, part in enumerate(parts):
                cols = pl.ds(i * width, width)
                scaled = part * factor * gain[:, cols].astype(F32)
                normed[pl.ds(low_here, 16), cols] = scaled.astype(BF16)
            return carry

        if block == 0:
            w_copies[2].wait()
        lax.fori_loop(0, BLOCK // 16, norm_rows, 0)
        if block == 0:
            w_copies[1].wait()
        made = jnp.dot(normed[...], wkv[...], preferred_element_type=F32)
        kv_own[pl.ds(block * BLOCK, BLOCK), :] = made.astype(BF16)
        k_start(block)
        if block == 0:
            w_copies[0].wait()

        def query_tile(n, carry):
            cols = pl.ds(pl.multiple_of(n * 256, 256), 256)
            tile = jnp.dot(normed[...], wq[:, cols], preferred_element_type=F32).astype(BF16)
            q_out[block, 2 * n] = tile[:, :HEAD]
            q_out[block, 2 * n + 1] = tile[:, HEAD:]
            return carry

        lax.fori_loop(0, wq.shape[1] // 256, query_tile, 0)

    for way in range(2):
        z_go(0, way, 0)
    for way in range(2):
        z_go(0, way, 1)
    go(remote(cache, cached_at(rank, 0, span), y, 0, (s, up, t)))
    go(remote(cache, cached_at(rank, 0, span), y, 1, (s, down, t)))
    go(remote(cache, cached_at(rank, 0, span), y, 4, (s, twin, t)))
    reset_state(m_s, l_s, acc_s)
    layout = Layout(cache_len, row_len, n_docs)
    first = rank * held
    c_low, c_high, r_low = layout.ranges(first, first + BLOCK - 1)
    row = lane_rows(first)
    lane_low, lane_high, lane_r_low = layout.ranges(row, row)

    for way in range(2):
        z_take(0, way, 0)
        z_go(0, way, 2)
    for way in range(2):
        z_go(1, way, 0)
    for way in range(2):
        z_go(1, way, 1)
    own_tok.wait()
    for way in range(2):
        z_take(0, way, 1)
        z_take(0, way, 2)
    y_take(0, down, 0, span)
    y_go(2, down, 0, mid, up)
    y_go(5, down, 0, span, twin)
    y_take(1, up, 0, span)
    y_go(3, up, mid, span, down)
    y_go(6, up, 0, span, twin)
    project_block(0)
    for way in range(2):
        z_take(1, way, 0)
        z_go(1, way, 2)
    y_take(2, across, 0, mid)
    y_go(7, across, 0, mid, twin)
    y_take(3, across, mid, span)
    y_go(8, across, mid, span, twin)
    k_pass_on(0)
    own_cache.wait()
    y_take(4, twin, 0, span)
    y_take(5, twin_of(down), 0, span)
    y_take(6, twin_of(up), 0, span)
    y_take(7, twin_of(across), 0, mid)
    y_take(8, twin_of(across), mid, span)

    def early(c, carry):
        queries = [q_out[0, h] for h in range(heads)]
        start = align_down(c_low) + c * CHUNK
        attend_chunk(cache_all, start, CHUNK, lane_low, lane_high, queries, m_s, l_s, acc_s)
        return carry

    lax.fori_loop(0, EARLY // 2, early, 0)
    for way in range(2):
        z_take(1, way, 1)
        z_take(1, way, 2)
    project_block(1)
    own_kv = pltpu.make_async_copy(
        kv_own, kv_all.at[pl.ds(pl.multiple_of(rank * held, held), held)], loc_sem.at[1]
    )
    own_kv.start()
    lax.fori_loop(EARLY // 2, EARLY - 1, early, 0)
    k_pass_on(1)
    lax.fori_loop(EARLY - 1, EARLY, early, 0)
    for block in range(2):
        k_finish(block)
    own_kv.wait()
    for copy in started:
        copy.wait_send()


def project(own_rows, gain, w_query, w_kv, cache, cache_len, row_len, n_dp, n_t):
    rows, width = own_rows.shape
    blocks = rows // BLOCK
    full, heads_width = w_query.shape
    kv_width = w_kv.shape[1]
    heads = heads_width // HEAD
    span = cache.shape[0]
    vmem = pl.BlockSpec(memory_space=pltpu.VMEM)
    smem = pl.BlockSpec(memory_space=pltpu.SMEM)
    hbm = pl.BlockSpec(memory_space=pltpu.HBM)
    large = (own_rows, gain, w_query, w_kv, cache)
    return pl.pallas_call(
        functools.partial(project_kernel, n_dp, n_t, cache_len.shape[1]),
        out_shape=(
            jax.ShapeDtypeStruct((blocks, heads, BLOCK, HEAD), BF16),
            jax.ShapeDtypeStruct((n_dp * span, kv_width), BF16),
            jax.ShapeDtypeStruct((n_dp * rows, kv_width), BF16),
            jax.ShapeDtypeStruct((1, heads * BLOCK), F32),
            jax.ShapeDtypeStruct((1, heads * BLOCK), F32),
            jax.ShapeDtypeStruct((HEAD, heads * BLOCK), F32),
        ),
        in_specs=[hbm] * len(large) + [smem] * 2,
        out_specs=(vmem,) * 6,
        scratch_shapes=[
            pltpu.VMEM((n_t, rows, width), BF16),
            pltpu.VMEM(gain.shape, BF16),
            pltpu.VMEM((full, heads_width), BF16),
            pltpu.VMEM((full, kv_width), BF16),
            pltpu.VMEM((BLOCK, full), BF16),
            pltpu.VMEM((rows, kv_width), BF16),
            pltpu.SemaphoreType.DMA((3,)),
            pltpu.SemaphoreType.DMA((3,)),
            pltpu.SemaphoreType.DMA((12,)),
            pltpu.SemaphoreType.DMA((12,)),
            pltpu.SemaphoreType.DMA((9,)),
            pltpu.SemaphoreType.DMA((9,)),
            pltpu.SemaphoreType.DMA((14,)),
            pltpu.SemaphoreType.DMA((14,)),
        ],
        compiler_params=pltpu.CompilerParams(
            collective_id=0, has_side_effects=True, vmem_limit_bytes=32 * 1024 * 1024
        ),
        name="project",
    )(*(pltpu.with_memory_space_constraint(a, pltpu.HBM) for a in large + (cache_len, row_len)))


def attend_kernel(
    n_docs, cache_len, row_len, owner, q, cache, kv, m_in, l_in, acc_in,
    out, held, m_s, l_s, acc_s,
):
    rank = lax.axis_index("dp")
    blocks, heads = q.shape[:2]
    layout = Layout(cache_len, row_len, n_docs)

    def one_block(block, carry):
        first = (rank * blocks + block) * BLOCK
        c_low, c_high, r_low = layout.ranges(first, first + BLOCK - 1)
        row = lane_rows(first)
        row_c_low, row_c_high, row_r_low = layout.ranges(row, row)
        queries = [q[block, h] for h in range(heads)]

        @pl.when(block == 0)
        def _():
            m_s[...] = m_in[...]
            l_s[...] = l_in[...]
            acc_s[...] = acc_in[...]

        @pl.when(block > 0)
        def _():
            reset_state(m_s, l_s, acc_s)

        def one_range(source, low, high, lane_low, lane_high, done):
            begin = align_down(low)
            total = high - begin
            whole = total // CHUNK
            rest = total - whole * CHUNK

            def one(c, carry):
                start = begin + c * CHUNK
                attend_chunk(source, start, CHUNK, lane_low, lane_high, queries, m_s, l_s, acc_s)
                return carry

            lax.fori_loop(done, whole + (rest > CHUNK // 2).astype(jnp.int32), one, 0)

            @pl.when((rest > 0) & (rest <= CHUNK // 2) & (whole >= done))
            def _():
                start = begin + whole * CHUNK
                attend_chunk(
                    source, start, CHUNK // 2, lane_low, lane_high, queries, m_s, l_s, acc_s
                )

        done = jnp.where(block == 0, EARLY, LATE)
        one_range(cache, c_low, c_high, row_c_low, row_c_high, done)

        @pl.when(block == 0)
        def _():
            one_range(kv, r_low, first + BLOCK, row_r_low, row + 1, 0)
            finish_block(heads, out, m_s, l_s, acc_s)

        return carry

    lax.fori_loop(0, blocks, one_block, 0)

    def load_of(b, total):
        low = b * BLOCK
        work = low * BLOCK + (BLOCK * (BLOCK - 1)) // 2
        for d in range(n_docs):
            inside = jnp.minimum(layout.r_end[d], low + BLOCK) - jnp.maximum(layout.r_start[d], low)
            gain = layout.c_len[d] - layout.r_start[d] + 1
            work = work + jnp.maximum(inside, 0) * gain
        return total + jnp.where(owner[b] == rank, work, 0)

    total = lax.fori_loop(0, owner.shape[0], load_of, jnp.int32(0))
    held[0, 0] = total.astype(F32) * (2.0 / (BLOCK * (cache.shape[0] + kv.shape[0])))


def attend(cache_len, row_len, owner, q, cache, kv, state):
    blocks, heads = q.shape[:2]
    vmem = pl.BlockSpec(memory_space=pltpu.VMEM)
    smem = pl.BlockSpec(memory_space=pltpu.SMEM)
    return pl.pallas_call(
        functools.partial(attend_kernel, cache_len.shape[1]),
        out_shape=(
            jax.ShapeDtypeStruct((BLOCK, heads * HEAD), BF16),
            jax.ShapeDtypeStruct((1, 1), F32),
        )
        + tuple(jax.ShapeDtypeStruct(part.shape, F32) for part in state),
        in_specs=[smem] * 3 + [vmem] * 6,
        out_specs=(vmem, smem) + (vmem,) * 3,
        compiler_params=pltpu.CompilerParams(vmem_limit_bytes=32 * 1024 * 1024),
        name="attend",
    )(cache_len, row_len, owner, q, cache, kv, *state)


PIECES = 2


def output_kernel(
    n_pipe, n_t, n_docs, cache_len, row_len, att0, tok, wo, q, cache, kv, m_in, l_in, acc_in, out,
    m_s, l_s, acc_s, att1, far, far_in, to_right, to_left, own, sent, from_left, from_right, section,
    z_send, z_recv, x_send, x_recv,
):
    s = lax.axis_index("pipe")
    rank = lax.axis_index("dp")
    t = lax.axis_index("tensor")
    right, left = lax.rem(t + 1, n_t), lax.rem(t + n_t - 1, n_t)
    over = lax.rem(t + 2, n_t)
    ahead, behind = lax.rem(s + 1, n_pipe), lax.rem(s + n_pipe - 1, n_pipe)
    z, x = (z_send, z_recv), (x_send, x_recv)
    width = tok.shape[1]
    size = BLOCK // PIECES
    half = size // 2
    blocks, heads = q.shape[:2]

    barrier = pltpu.get_barrier_semaphore()
    for other in (left, right):
        pl.semaphore_signal(barrier, inc=1, device_id=(s, rank, other), device_id_type=MESH)
    for other in (ahead, behind):
        pl.semaphore_signal(barrier, inc=1, device_id=(other, rank, t), device_id_type=MESH)

    def multiply(att, target, store):
        def tile(n, carry):
            cols = pl.ds(pl.multiple_of(n * 256, 256), 256)
            out_cols = pl.ds(pl.multiple_of(target * width + n * 256, 256), 256)
            store(cols, jnp.dot(att[...], wo[:, out_cols], preferred_element_type=F32))
            return carry

        lax.fori_loop(0, width // 256, tile, 0)

    started = []

    def go(copy):
        copy.start()
        started.append(copy)

    def span(p, way):
        return pl.ds(p * size + way * half, half)

    def local(p, way):
        return pl.ds(p % PIECES * size + way * half, half)

    def far_copy(p, way):
        target = right if way == 0 else left
        part = span(p, way)
        return remote(far.at[part], far_in.at[part], z, p * 6 + way, (s, rank, target))

    def near_copy(p, way, kind):
        part = span(p, way if kind == 1 else 1 - way)
        target, box = (right, from_left) if way == 0 else (left, from_right)
        index = p * 6 + 2 + 2 * kind + way
        return remote(sent.at[way, part], box.at[part], z, index, (s, rank, target))

    held = (to_right, to_left)

    def pieces(block):
        return range(block * PIECES, block * PIECES + PIECES)

    def block_rows(block):
        return pl.ds(block * BLOCK, BLOCK)

    def multiply_far(block, att):
        def store_far(cols, value):
            far[block_rows(block), cols] = value.astype(BF16)

        multiply(att, over, store_far)

    def send_far(block):
        for p in pieces(block):
            for way in range(2):
                go(far_copy(p, way))

    def multiply_near(block, att):
        def store_right(cols, value):
            to_right[:, cols] = value

        def store_left(cols, value):
            to_left[:, cols] = value

        multiply(att, right, store_right)
        multiply(att, left, store_left)

    def multiply_own(block, att):
        def store_own(cols, value):
            own[:, cols] = value + tok[block_rows(block), cols].astype(F32)

        multiply(att, t, store_own)

    def send_free(p):
        for way in range(2):
            sent[way, span(p, 1 - way), :] = held[way][local(p, 1 - way), :].astype(BF16)
            go(near_copy(p, way, 0))

    def send_merged(p):
        for way in range(2):
            part = span(p, way)
            far_copy(p, way).wait_recv()
            both = held[way][local(p, way), :] + far_in[part, :].astype(F32)
            sent[way, part, :] = both.astype(BF16)
            go(near_copy(p, way, 1))

    def finish(p):
        for way in range(2):
            near_copy(p, way, 0).wait_recv()
            near_copy(p, way, 1).wait_recv()
        part = pl.ds(p * size, size)
        total = from_left[part, :].astype(F32) + from_right[part, :].astype(F32)
        mine = own[pl.ds(p % PIECES * size, size), :]
        section[part, :] = (mine + total).astype(BF16)
        go(remote(section.at[part], out.at[part], x, p, (ahead, rank, t)))

    first = (rank * blocks + 1) * BLOCK
    layout = Layout(cache_len, row_len, n_docs)
    c_low, c_high, r_low = layout.ranges(first, first + BLOCK - 1)
    row = lane_rows(first)
    row_c_low, row_c_high, row_r_low = layout.ranges(row, row)

    def cached(c, carry):
        queries = [q[1, h] for h in range(heads)]
        start = align_down(c_low) + c * CHUNK
        attend_chunk(cache, start, CHUNK, row_c_low, row_c_high, queries, m_s, l_s, acc_s)
        return carry

    def fresh(start, amount):
        queries = [q[1, h] for h in range(heads)]
        attend_chunk(kv, start, amount, row_r_low, row + 1, queries, m_s, l_s, acc_s)

    multiply_far(0, att0)
    pl.semaphore_wait(barrier, 4)
    send_far(0)
    multiply_near(0, att0)
    for p in pieces(0):
        send_free(p)
    multiply_own(0, att0)
    m_s[...] = m_in[...]
    l_s[...] = l_in[...]
    acc_s[...] = acc_in[...]
    lax.fori_loop(0, 1, cached, 0)
    for p in pieces(0):
        send_merged(p)
    lax.fori_loop(1, LATE, cached, 0)
    finish(0)
    begin = align_down(r_low)
    fresh(begin, CHUNK)
    fresh(begin + CHUNK, 2 * BLOCK)
    finish_block(heads, att1, m_s, l_s, acc_s)
    multiply_far(1, att1)
    send_far(1)
    for p in pieces(0):
        if p > 0:
            finish(p)
    multiply_near(1, att1)
    for p in pieces(1):
        send_free(p)
        send_merged(p)
    multiply_own(1, att1)
    for p in pieces(1):
        finish(p)
    for p in range(blocks * PIECES):
        part = pl.ds(p * size, size)
        remote(section.at[part], out.at[part], x, p, (ahead, rank, t)).wait_recv()
    for copy in started:
        copy.wait_send()


def output(cache_len, row_len, att, own_rows, w_out, q, cache, kv, state, n_pipe, n_t):
    rows, width = own_rows.shape
    copies = rows // BLOCK * PIECES
    vmem = pl.BlockSpec(memory_space=pltpu.VMEM)
    smem = pl.BlockSpec(memory_space=pltpu.SMEM)
    whole, one = (rows, width), (BLOCK, width)
    return pl.pallas_call(
        functools.partial(output_kernel, n_pipe, n_t, cache_len.shape[1]),
        out_shape=jax.ShapeDtypeStruct(whole, BF16),
        in_specs=[smem] * 2 + [vmem] * 9,
        out_specs=pl.BlockSpec(memory_space=pl.ANY),
        scratch_shapes=[pltpu.VMEM(part.shape, F32) for part in state]
        + [
            pltpu.VMEM(att.shape, BF16),
            pltpu.VMEM(whole, BF16),
            pltpu.VMEM(whole, BF16),
            pltpu.VMEM(one, F32),
            pltpu.VMEM(one, F32),
            pltpu.VMEM(one, F32),
            pltpu.VMEM((2,) + whole, BF16),
            pltpu.VMEM(whole, BF16),
            pltpu.VMEM(whole, BF16),
            pltpu.VMEM(whole, BF16),
            pltpu.SemaphoreType.DMA((6 * copies,)),
            pltpu.SemaphoreType.DMA((6 * copies,)),
            pltpu.SemaphoreType.DMA((copies,)),
            pltpu.SemaphoreType.DMA((copies,)),
        ],
        compiler_params=pltpu.CompilerParams(
            collective_id=1, has_side_effects=True, vmem_limit_bytes=32 * 1024 * 1024
        ),
        name="output",
    )(cache_len, row_len, att, own_rows, w_out, q, cache, kv, *state)


def on_device(
    tokens, norm_gain, w_query, key_value_weight, w_out, cache_kv,
    cache_lengths, row_lengths, block_owner,
):
    n_pipe, n_dp, n_t = (lax.axis_size(a) for a in ("pipe", "dp", "tensor"))
    own_rows = tokens[0]
    span = cache_kv.shape[1]
    cache = cache_kv.reshape(span, cache_kv.shape[3])
    q, cache_all, kv_all, *state = project(
        own_rows, norm_gain, w_query[0], key_value_weight[0], cache,
        cache_lengths, row_lengths, n_dp, n_t,
    )
    owner = block_owner.reshape(-1)
    att, held, *state = attend(
        cache_lengths, row_lengths, owner, q, cache_all, kv_all, state
    )
    handed = output(
        cache_lengths, row_lengths, att, own_rows, w_out[0], q, cache_all, kv_all, state, n_pipe, n_t
    )
    return handed[None], held


def solution(mesh):
    placed = (
        P("pipe", "dp", "tensor"),
        P("pipe", None),
        P("pipe", None, "tensor"),
        P("pipe", None, "tensor"),
        P("pipe", "tensor", None),
        P("pipe", "dp", "tensor", None),
        P("pipe", None),
        P("pipe", None),
        P("pipe", None, None),
    )
    return jax.shard_map(
        on_device,
        mesh=mesh,
        in_specs=placed,
        out_specs=(P("pipe", "dp", "tensor"), P("pipe", "dp")),
        check_vma=False,
    )
```

```python
import functools

import jax
import jax.numpy as jnp
from jax import lax
from jax.experimental import pallas as pl
from jax.experimental.pallas import tpu as pltpu
from jax.sharding import PartitionSpec as P

HEAD = 128
BLOCK = 128
EPS = 1e-06
NEG = -1e30
LOG2E = 1.4426950408889634
MESH = pl.DeviceIdType.MESH
F32 = jnp.float32
BF16 = jnp.bfloat16


def remote(src, dst, sems, index, target):
    return pltpu.make_async_remote_copy(
        src_ref=src,
        dst_ref=dst,
        send_sem=sems[0].at[index],
        recv_sem=sems[1].at[index],
        device_id=target,
        device_id_type=MESH,
    )


class Layout:
    def __init__(self, cache_len, row_len, n_docs):
        self.n = n_docs
        self.c_len = [cache_len[0, d] for d in range(n_docs)]
        self.r_len = [row_len[0, d] for d in range(n_docs)]
        self.r_start, self.r_end = [], []
        total = jnp.int32(0)
        for length in self.r_len:
            self.r_start.append(total)
            total = total + length
            self.r_end.append(total)

    def _sum(self, tests, values):
        total = jnp.where(tests[0], values[0], 0)
        for test, value in zip(tests[1:], values[1:]):
            total = total + jnp.where(test, value, 0)
        return total

    def ranges(self, first, last):
        past = [end <= first for end in self.r_end]
        begun = [start <= last for start in self.r_start]
        return self._sum(past, self.c_len), self._sum(begun, self.c_len), self._sum(past, self.r_len)


def lane_rows(first):
    return first + lax.broadcasted_iota(jnp.int32, (1, BLOCK), 1)


def align_down(value):
    return lax.div(value, 16) * 16


def reset_state(m_s, l_s, acc_s):
    m_s[...] = jnp.full(m_s.shape, NEG, F32)
    l_s[...] = jnp.zeros(l_s.shape, F32)
    acc_s[...] = jnp.zeros(acc_s.shape, F32)


def attend_chunk(hist, start, size, low, high, queries, m_s, l_s, acc_s):
    scale = HEAD ** (-0.5) * LOG2E
    place0 = jnp.minimum(lax.div(start, 16), (hist.shape[0] - size) // 16) * 16
    at = pl.ds(place0, size)
    keys = hist[at, :HEAD]
    values_t = hist[at, HEAD:].T
    place = place0 + lax.broadcasted_iota(jnp.int32, (size, BLOCK), 0)
    bias = jnp.where((place >= jnp.maximum(low, start)) & (place < high), 0.0, 2 * NEG)
    bias = jnp.concatenate([bias, bias], axis=1)
    heads = len(queries)
    scores = []
    for h in range(0, heads, 2):
        pair = jnp.concatenate([queries[h], queries[h + 1]], axis=0)
        scores.append(
            lax.dot_general(keys, pair, (((1,), (1,)), ((), ())), preferred_element_type=F32)
        )
    weighted = []
    for i, score in enumerate(scores):
        cols = pl.ds(i * 2 * BLOCK, 2 * BLOCK)
        score = score + bias
        prior = m_s[:, cols]
        newest = jnp.maximum(prior, jnp.max(score, axis=0, keepdims=True))
        weights = jnp.exp2((score - newest) * scale)
        rescale = jnp.exp2((prior - newest) * scale)
        m_s[:, cols] = newest
        l_s[:, cols] = l_s[:, cols] * rescale + jnp.sum(weights, axis=0, keepdims=True)
        weighted.append((weights.astype(BF16), rescale))
    for i, (weights, rescale) in enumerate(weighted):
        cols = pl.ds(i * 2 * BLOCK, 2 * BLOCK)
        product = jnp.dot(values_t, weights, preferred_element_type=F32)
        acc_s[:, cols] = acc_s[:, cols] * rescale + product


def finish_block(heads, out, m_s, l_s, acc_s):
    for h in range(heads):
        cols = pl.ds(h * BLOCK, BLOCK)
        out[:, cols] = (acc_s[:, cols] / l_s[:, cols]).T.astype(BF16)


CHUNK = 1024
EARLY = 4
LATE = 4

def project_kernel(
    n_dp, n_t, n_docs, tok, gain_hbm, wq_hbm, wkv_hbm, cache, cache_len, row_len,
    q_out, cache_all, kv_all, m_s, l_s, acc_s,
    xs, gain, wq, wkv, normed, kv_own, w_sem, loc_sem,
    z_send, z_recv, y_send, y_recv, k_send, k_recv,
):
    s = lax.axis_index("pipe")
    rank = lax.axis_index("dp")
    t = lax.axis_index("tensor")
    right, left = lax.rem(t + 1, n_t), lax.rem(t + n_t - 1, n_t)
    over = lax.rem(t + 2, n_t)
    up, down = lax.rem(rank + 2, n_dp), lax.rem(rank + n_dp - 2, n_dp)
    across = lax.rem(rank + 4, n_dp)

    def twin_of(r):
        return r + 1 - 2 * lax.rem(r, 2)

    twin = twin_of(rank)
    z, y, k = (z_send, z_recv), (y_send, y_recv), (k_send, k_recv)
    half = BLOCK // 2
    span = cache.shape[0]
    mid = span // 2
    held = kv_own.shape[0]
    heads = q_out.shape[1]

    def cached_at(slot, lower, upper):
        return cache_all.at[pl.ds(pl.multiple_of(slot * span + lower, mid), upper - lower)]

    def fresh_at(slot, block):
        return kv_all.at[pl.ds(pl.multiple_of(slot * held + block * BLOCK, BLOCK), BLOCK)]

    w_copies = [
        pltpu.make_async_copy(wq_hbm, wq, w_sem.at[0]),
        pltpu.make_async_copy(wkv_hbm, wkv, w_sem.at[1]),
        pltpu.make_async_copy(gain_hbm, gain, w_sem.at[2]),
    ]
    own_tok = pltpu.make_async_copy(tok, xs.at[t], loc_sem.at[2])
    own_cache = pltpu.make_async_copy(cache, cached_at(rank, 0, span), loc_sem.at[0])

    barrier = pltpu.get_barrier_semaphore()
    for other in (left, right):
        pl.semaphore_signal(barrier, inc=1, device_id=(s, rank, other), device_id_type=MESH)
    for other in (up, down, across, twin):
        pl.semaphore_signal(barrier, inc=1, device_id=(s, other, t), device_id_type=MESH)
    own_tok.start()
    own_cache.start()
    for copy in w_copies:
        copy.start()
    pl.semaphore_wait(barrier, 6)

    started = []

    def go(copy):
        copy.start()
        started.append(copy)

    def rows(block, way, kind):
        low = block * BLOCK + (half if (way == 0) == (kind == 1) else 0)
        return pl.ds(low, half)

    def z_go(block, way, kind):
        part = rows(block, way, kind)
        target, source = (right, left) if way == 0 else (left, right)
        slot = source if kind == 2 else t
        src = xs.at[slot, part] if kind == 2 else tok.at[part]
        index = block * 6 + way * 3 + kind
        go(remote(src, xs.at[slot, part], z, index, (s, rank, target)))

    def z_take(block, way, kind):
        source = left if way == 0 else right
        slot = over if kind == 2 else source
        here = xs.at[slot, rows(block, way, kind)]
        index = block * 6 + way * 3 + kind
        remote(here, here, z, index, (s, rank, source)).wait_recv()

    def y_take(index, slot, lower, upper):
        part = cached_at(slot, lower, upper)
        remote(part, part, y, index, (s, twin, t)).wait_recv()

    def y_go(index, slot, lower, upper, target):
        part = cached_at(slot, lower, upper)
        go(remote(part, part, y, index, (s, target, t)))

    def k_start(block):
        part = kv_own.at[pl.ds(block * BLOCK, BLOCK)]
        for i, target in enumerate((up, down, across, twin)):
            go(remote(part, fresh_at(rank, block), k, block * 7 + i, (s, target, t)))

    def k_take(index, slot, block):
        here = fresh_at(slot, block)
        remote(here, here, k, index, (s, twin, t)).wait_recv()

    def k_pass_on(block):
        for i, slot in enumerate((down, up, across)):
            k_take(block * 7 + i, slot, block)
            here = fresh_at(slot, block)
            go(remote(here, here, k, block * 7 + 4 + i, (s, twin, t)))

    def k_finish(block):
        k_take(block * 7 + 3, twin, block)
        for i, slot in enumerate((down, up, across)):
            k_take(block * 7 + 4 + i, twin_of(slot), block)

    def project_block(block):
        def norm_rows(step, carry):
            low = pl.multiple_of(block * BLOCK + step * 16, 16)
            low_here = pl.multiple_of(step * 16, 16)
            parts = [xs[i, pl.ds(low, 16), :].astype(F32) for i in range(n_t)]
            total = jnp.sum(parts[0] * parts[0], axis=1, keepdims=True)
            for part in parts[1:]:
                total += jnp.sum(part * part, axis=1, keepdims=True)
            width = parts[0].shape[1]
            factor = lax.rsqrt(total / (width * n_t) + EPS)
            for i, part in enumerate(parts):
                cols = pl.ds(i * width, width)
                scaled = part * factor * gain[:, cols].astype(F32)
                normed[pl.ds(low_here, 16), cols] = scaled.astype(BF16)
            return carry

        if block == 0:
            w_copies[2].wait()
        lax.fori_loop(0, BLOCK // 16, norm_rows, 0)
        if block == 0:
            w_copies[1].wait()
        made = jnp.dot(normed[...], wkv[...], preferred_element_type=F32)
        kv_own[pl.ds(block * BLOCK, BLOCK), :] = made.astype(BF16)
        k_start(block)
        if block == 0:
            w_copies[0].wait()

        def query_tile(n, carry):
            cols = pl.ds(pl.multiple_of(n * 256, 256), 256)
            tile = jnp.dot(normed[...], wq[:, cols], preferred_element_type=F32).astype(BF16)
            q_out[block, 2 * n] = tile[:, :HEAD]
            q_out[block, 2 * n + 1] = tile[:, HEAD:]
            return carry

        lax.fori_loop(0, wq.shape[1] // 256, query_tile, 0)

    for way in range(2):
        z_go(0, way, 0)
    for way in range(2):
        z_go(0, way, 1)
    go(remote(cache, cached_at(rank, 0, span), y, 0, (s, up, t)))
    go(remote(cache, cached_at(rank, 0, span), y, 1, (s, down, t)))
    go(remote(cache, cached_at(rank, 0, span), y, 4, (s, twin, t)))
    reset_state(m_s, l_s, acc_s)
    layout = Layout(cache_len, row_len, n_docs)
    first = rank * held
    c_low, c_high, r_low = layout.ranges(first, first + BLOCK - 1)
    row = lane_rows(first)
    lane_low, lane_high, lane_r_low = layout.ranges(row, row)

    for way in range(2):
        z_take(0, way, 0)
        z_go(0, way, 2)
    for way in range(2):
        z_go(1, way, 0)
    for way in range(2):
        z_go(1, way, 1)
    own_tok.wait()
    for way in range(2):
        z_take(0, way, 1)
        z_take(0, way, 2)
    y_take(0, down, 0, span)
    y_go(2, down, 0, mid, up)
    y_go(5, down, 0, span, twin)
    y_take(1, up, 0, span)
    y_go(3, up, mid, span, down)
    y_go(6, up, 0, span, twin)
    project_block(0)
    for way in range(2):
        z_take(1, way, 0)
        z_go(1, way, 2)
    y_take(2, across, 0, mid)
    y_go(7, across, 0, mid, twin)
    y_take(3, across, mid, span)
    y_go(8, across, mid, span, twin)
    own_cache.wait()
    y_take(4, twin, 0, span)
    y_take(5, twin_of(down), 0, span)
    y_take(6, twin_of(up), 0, span)
    y_take(7, twin_of(across), 0, mid)
    y_take(8, twin_of(across), mid, span)

    def early(c, carry):
        queries = [q_out[0, h] for h in range(heads)]
        start = align_down(c_low) + c * CHUNK
        attend_chunk(cache_all, start, CHUNK, lane_low, lane_high, queries, m_s, l_s, acc_s)
        return carry

    lax.fori_loop(0, EARLY // 2, early, 0)
    for way in range(2):
        z_take(1, way, 1)
        z_take(1, way, 2)
    project_block(1)
    own_kv = pltpu.make_async_copy(
        kv_own, kv_all.at[pl.ds(pl.multiple_of(rank * held, held), held)], loc_sem.at[1]
    )
    own_kv.start()
    lax.fori_loop(EARLY // 2, EARLY - 1, early, 0)
    k_pass_on(0)
    k_pass_on(1)
    lax.fori_loop(EARLY - 1, EARLY, early, 0)
    for block in range(2):
        k_finish(block)
    own_kv.wait()
    for copy in started:
        copy.wait_send()


def project(own_rows, gain, w_query, w_kv, cache, cache_len, row_len, n_dp, n_t):
    rows, width = own_rows.shape
    blocks = rows // BLOCK
    full, heads_width = w_query.shape
    kv_width = w_kv.shape[1]
    heads = heads_width // HEAD
    span = cache.shape[0]
    vmem = pl.BlockSpec(memory_space=pltpu.VMEM)
    smem = pl.BlockSpec(memory_space=pltpu.SMEM)
    hbm = pl.BlockSpec(memory_space=pltpu.HBM)
    large = (own_rows, gain, w_query, w_kv, cache)
    return pl.pallas_call(
        functools.partial(project_kernel, n_dp, n_t, cache_len.shape[1]),
        out_shape=(
            jax.ShapeDtypeStruct((blocks, heads, BLOCK, HEAD), BF16),
            jax.ShapeDtypeStruct((n_dp * span, kv_width), BF16),
            jax.ShapeDtypeStruct((n_dp * rows, kv_width), BF16),
            jax.ShapeDtypeStruct((1, heads * BLOCK), F32),
            jax.ShapeDtypeStruct((1, heads * BLOCK), F32),
            jax.ShapeDtypeStruct((HEAD, heads * BLOCK), F32),
        ),
        in_specs=[hbm] * len(large) + [smem] * 2,
        out_specs=(vmem,) * 6,
        scratch_shapes=[
            pltpu.VMEM((n_t, rows, width), BF16),
            pltpu.VMEM(gain.shape, BF16),
            pltpu.VMEM((full, heads_width), BF16),
            pltpu.VMEM((full, kv_width), BF16),
            pltpu.VMEM((BLOCK, full), BF16),
            pltpu.VMEM((rows, kv_width), BF16),
            pltpu.SemaphoreType.DMA((3,)),
            pltpu.SemaphoreType.DMA((3,)),
            pltpu.SemaphoreType.DMA((12,)),
            pltpu.SemaphoreType.DMA((12,)),
            pltpu.SemaphoreType.DMA((9,)),
            pltpu.SemaphoreType.DMA((9,)),
            pltpu.SemaphoreType.DMA((14,)),
            pltpu.SemaphoreType.DMA((14,)),
        ],
        compiler_params=pltpu.CompilerParams(
            collective_id=0, has_side_effects=True, vmem_limit_bytes=32 * 1024 * 1024
        ),
        name="project",
    )(*(pltpu.with_memory_space_constraint(a, pltpu.HBM) for a in large + (cache_len, row_len)))


def attend_kernel(
    n_docs, cache_len, row_len, owner, q, cache, kv, m_in, l_in, acc_in,
    out, held, m_s, l_s, acc_s,
):
    rank = lax.axis_index("dp")
    blocks, heads = q.shape[:2]
    layout = Layout(cache_len, row_len, n_docs)

    def one_block(block, carry):
        first = (rank * blocks + block) * BLOCK
        c_low, c_high, r_low = layout.ranges(first, first + BLOCK - 1)
        row = lane_rows(first)
        row_c_low, row_c_high, row_r_low = layout.ranges(row, row)
        queries = [q[block, h] for h in range(heads)]

        @pl.when(block == 0)
        def _():
            m_s[...] = m_in[...]
            l_s[...] = l_in[...]
            acc_s[...] = acc_in[...]

        @pl.when(block > 0)
        def _():
            reset_state(m_s, l_s, acc_s)

        def one_range(source, low, high, lane_low, lane_high, done):
            begin = align_down(low)
            total = high - begin
            whole = total // CHUNK
            rest = total - whole * CHUNK

            def one(c, carry):
                start = begin + c * CHUNK
                attend_chunk(source, start, CHUNK, lane_low, lane_high, queries, m_s, l_s, acc_s)
                return carry

            lax.fori_loop(done, whole + (rest > CHUNK // 2).astype(jnp.int32), one, 0)

            start = begin + whole * CHUNK

            def remainder(size):
                attend_chunk(source, start, size, lane_low, lane_high, queries, m_s, l_s, acc_s)

            left = (rest <= CHUNK // 2) & (whole >= done)
            pl.when(left & (rest > BLOCK))(lambda: remainder(CHUNK // 2))
            pl.when(left & (rest > 0) & (rest <= BLOCK))(lambda: remainder(BLOCK))

        done = jnp.where(block == 0, EARLY, LATE)
        one_range(cache, c_low, c_high, row_c_low, row_c_high, done)

        @pl.when(block == 0)
        def _():
            one_range(kv, r_low, first + BLOCK, row_r_low, row + 1, 0)
            finish_block(heads, out, m_s, l_s, acc_s)

        return carry

    lax.fori_loop(0, blocks, one_block, 0)

    def load_of(b, total):
        low = b * BLOCK
        work = low * BLOCK + (BLOCK * (BLOCK - 1)) // 2
        for d in range(n_docs):
            inside = jnp.minimum(layout.r_end[d], low + BLOCK) - jnp.maximum(layout.r_start[d], low)
            gain = layout.c_len[d] - layout.r_start[d] + 1
            work = work + jnp.maximum(inside, 0) * gain
        return total + jnp.where(owner[b] == rank, work, 0)

    total = lax.fori_loop(0, owner.shape[0], load_of, jnp.int32(0))
    held[0, 0] = total.astype(F32) * (2.0 / (BLOCK * (cache.shape[0] + kv.shape[0])))


def attend(cache_len, row_len, owner, q, cache, kv, state):
    blocks, heads = q.shape[:2]
    vmem = pl.BlockSpec(memory_space=pltpu.VMEM)
    smem = pl.BlockSpec(memory_space=pltpu.SMEM)
    return pl.pallas_call(
        functools.partial(attend_kernel, cache_len.shape[1]),
        out_shape=(
            jax.ShapeDtypeStruct((BLOCK, heads * HEAD), BF16),
            jax.ShapeDtypeStruct((1, 1), F32),
        )
        + tuple(jax.ShapeDtypeStruct(part.shape, F32) for part in state),
        in_specs=[smem] * 3 + [vmem] * 6,
        out_specs=(vmem, smem) + (vmem,) * 3,
        compiler_params=pltpu.CompilerParams(vmem_limit_bytes=32 * 1024 * 1024),
        name="attend",
    )(cache_len, row_len, owner, q, cache, kv, *state)


PIECES = 4


def output_kernel(
    n_pipe, n_t, n_docs, cache_len, row_len, att0, tok, wo, q, cache, kv, m_in, l_in, acc_in, out,
    m_s, l_s, acc_s, att1, far, far_in, to_right, to_left, own, sent, from_left, from_right, section,
    z_send, z_recv, x_send, x_recv,
):
    s = lax.axis_index("pipe")
    rank = lax.axis_index("dp")
    t = lax.axis_index("tensor")
    right, left = lax.rem(t + 1, n_t), lax.rem(t + n_t - 1, n_t)
    over = lax.rem(t + 2, n_t)
    ahead, behind = lax.rem(s + 1, n_pipe), lax.rem(s + n_pipe - 1, n_pipe)
    z, x = (z_send, z_recv), (x_send, x_recv)
    width = tok.shape[1]
    size = BLOCK // PIECES
    half = size // 2
    blocks, heads = q.shape[:2]

    barrier = pltpu.get_barrier_semaphore()
    for other in (left, right):
        pl.semaphore_signal(barrier, inc=1, device_id=(s, rank, other), device_id_type=MESH)
    for other in (ahead, behind):
        pl.semaphore_signal(barrier, inc=1, device_id=(other, rank, t), device_id_type=MESH)

    def multiply(att, target, store):
        def tile(n, carry):
            cols = pl.ds(pl.multiple_of(n * 256, 256), 256)
            out_cols = pl.ds(pl.multiple_of(target * width + n * 256, 256), 256)
            store(cols, jnp.dot(att[...], wo[:, out_cols], preferred_element_type=F32))
            return carry

        lax.fori_loop(0, width // 256, tile, 0)

    started = []

    def go(copy):
        copy.start()
        started.append(copy)

    def span(p, way):
        return pl.ds(p * size + way * half, half)

    def local(p, way):
        return pl.ds(p % PIECES * size + way * half, half)

    def far_copy(p, way):
        target = right if way == 0 else left
        part = span(p, way)
        return remote(far.at[part], far_in.at[part], z, p * 6 + way, (s, rank, target))

    def near_copy(p, way, kind):
        part = span(p, way if kind == 1 else 1 - way)
        target, box = (right, from_left) if way == 0 else (left, from_right)
        index = p * 6 + 2 + 2 * kind + way
        return remote(sent.at[way, part], box.at[part], z, index, (s, rank, target))

    held = (to_right, to_left)

    def pieces(block):
        return range(block * PIECES, block * PIECES + PIECES)

    def block_rows(block):
        return pl.ds(block * BLOCK, BLOCK)

    def multiply_far(block, att):
        def store_far(cols, value):
            far[block_rows(block), cols] = value.astype(BF16)

        multiply(att, over, store_far)

    def send_far(block):
        for p in pieces(block):
            for way in range(2):
                go(far_copy(p, way))

    def multiply_near(block, att):
        def store_right(cols, value):
            to_right[:, cols] = value

        def store_left(cols, value):
            to_left[:, cols] = value

        multiply(att, right, store_right)
        multiply(att, left, store_left)

    def multiply_own(block, att):
        def store_own(cols, value):
            own[:, cols] = value + tok[block_rows(block), cols].astype(F32)

        multiply(att, t, store_own)

    def send_free(p):
        for way in range(2):
            sent[way, span(p, 1 - way), :] = held[way][local(p, 1 - way), :].astype(BF16)
            go(near_copy(p, way, 0))

    def send_merged(p):
        for way in range(2):
            part = span(p, way)
            far_copy(p, way).wait_recv()
            both = held[way][local(p, way), :] + far_in[part, :].astype(F32)
            sent[way, part, :] = both.astype(BF16)
            go(near_copy(p, way, 1))

    def finish(p):
        for way in range(2):
            near_copy(p, way, 0).wait_recv()
            near_copy(p, way, 1).wait_recv()
        part = pl.ds(p * size, size)
        total = from_left[part, :].astype(F32) + from_right[part, :].astype(F32)
        mine = own[pl.ds(p % PIECES * size, size), :]
        section[part, :] = (mine + total).astype(BF16)
        go(remote(section.at[part], out.at[part], x, p, (ahead, rank, t)))

    first = (rank * blocks + 1) * BLOCK
    layout = Layout(cache_len, row_len, n_docs)
    c_low, c_high, r_low = layout.ranges(first, first + BLOCK - 1)
    row = lane_rows(first)
    row_c_low, row_c_high, row_r_low = layout.ranges(row, row)

    def cached(c, carry):
        queries = [q[1, h] for h in range(heads)]
        start = align_down(c_low) + c * CHUNK
        attend_chunk(cache, start, CHUNK, row_c_low, row_c_high, queries, m_s, l_s, acc_s)
        return carry

    def fresh(start, amount):
        queries = [q[1, h] for h in range(heads)]
        attend_chunk(kv, start, amount, row_r_low, row + 1, queries, m_s, l_s, acc_s)

    multiply_far(0, att0)
    pl.semaphore_wait(barrier, 4)
    send_far(0)
    multiply_near(0, att0)
    for p in pieces(0):
        send_free(p)
    multiply_own(0, att0)
    m_s[...] = m_in[...]
    l_s[...] = l_in[...]
    acc_s[...] = acc_in[...]
    lax.fori_loop(0, 1, cached, 0)
    for p in pieces(0):
        send_merged(p)
    lax.fori_loop(1, LATE, cached, 0)
    finish(0)
    begin = align_down(r_low)
    fresh(begin, CHUNK)
    fresh(begin + CHUNK, 2 * BLOCK)
    finish_block(heads, att1, m_s, l_s, acc_s)
    multiply_far(1, att1)
    send_far(1)
    for p in pieces(0):
        if p > 0:
            finish(p)
    multiply_near(1, att1)
    for p in pieces(1):
        send_free(p)
        send_merged(p)
    multiply_own(1, att1)
    for p in pieces(1):
        finish(p)
    for p in range(blocks * PIECES):
        part = pl.ds(p * size, size)
        remote(section.at[part], out.at[part], x, p, (ahead, rank, t)).wait_recv()
    for copy in started:
        copy.wait_send()


def output(cache_len, row_len, att, own_rows, w_out, q, cache, kv, state, n_pipe, n_t):
    rows, width = own_rows.shape
    copies = rows // BLOCK * PIECES
    vmem = pl.BlockSpec(memory_space=pltpu.VMEM)
    smem = pl.BlockSpec(memory_space=pltpu.SMEM)
    whole, one = (rows, width), (BLOCK, width)
    return pl.pallas_call(
        functools.partial(output_kernel, n_pipe, n_t, cache_len.shape[1]),
        out_shape=jax.ShapeDtypeStruct(whole, BF16),
        in_specs=[smem] * 2 + [vmem] * 9,
        out_specs=pl.BlockSpec(memory_space=pl.ANY),
        scratch_shapes=[pltpu.VMEM(part.shape, F32) for part in state]
        + [
            pltpu.VMEM(att.shape, BF16),
            pltpu.VMEM(whole, BF16),
            pltpu.VMEM(whole, BF16),
            pltpu.VMEM(one, F32),
            pltpu.VMEM(one, F32),
            pltpu.VMEM(one, F32),
            pltpu.VMEM((2,) + whole, BF16),
            pltpu.VMEM(whole, BF16),
            pltpu.VMEM(whole, BF16),
            pltpu.VMEM(whole, BF16),
            pltpu.SemaphoreType.DMA((6 * copies,)),
            pltpu.SemaphoreType.DMA((6 * copies,)),
            pltpu.SemaphoreType.DMA((copies,)),
            pltpu.SemaphoreType.DMA((copies,)),
        ],
        compiler_params=pltpu.CompilerParams(
            collective_id=1, has_side_effects=True, vmem_limit_bytes=32 * 1024 * 1024
        ),
        name="output",
    )(cache_len, row_len, att, own_rows, w_out, q, cache, kv, *state)


def on_device(
    tokens, norm_gain, w_query, key_value_weight, w_out, cache_kv,
    cache_lengths, row_lengths, block_owner,
):
    n_pipe, n_dp, n_t = (lax.axis_size(a) for a in ("pipe", "dp", "tensor"))
    own_rows = tokens[0]
    span = cache_kv.shape[1]
    cache = cache_kv.reshape(span, cache_kv.shape[3])
    q, cache_all, kv_all, *state = project(
        own_rows, norm_gain, w_query[0], key_value_weight[0], cache,
        cache_lengths, row_lengths, n_dp, n_t,
    )
    owner = block_owner.reshape(-1)
    att, held, *state = attend(
        cache_lengths, row_lengths, owner, q, cache_all, kv_all, state
    )
    handed = output(
        cache_lengths, row_lengths, att, own_rows, w_out[0], q, cache_all, kv_all, state, n_pipe, n_t
    )
    return handed[None], held


def solution(mesh):
    placed = (
        P("pipe", "dp", "tensor"),
        P("pipe", None),
        P("pipe", None, "tensor"),
        P("pipe", None, "tensor"),
        P("pipe", "tensor", None),
        P("pipe", "dp", "tensor", None),
        P("pipe", None),
        P("pipe", None),
        P("pipe", None, None),
    )
    return jax.shard_map(
        on_device,
        mesh=mesh,
        in_specs=placed,
        out_specs=(P("pipe", "dp", "tensor"), P("pipe", "dp")),
        check_vma=False,
    )
```
